32 devices in a mesh: expert: 2 (over x), dp: 16 (over z, y, core).
Axes of the slice: x: 2, y: 2, z: 4, core: 2. Of those that a mesh axis runs over, the one named last changes fastest.
Arguments:
- tokens: bfloat16 [384, 4096], P('expert'), may hold values from -6 to 6
- grad_out: bfloat16 [384, 4096], P('expert'), may hold values from -3 to 3
- gate_probs: bfloat16 [384, 2], P('expert'), may hold values from 0.19921875 to 1
- expert_ids: int32 [384, 2], P('expert'), may hold values from 0 to 3, all different within a row; in each aligned block of 192 rows (0 to 191, 192 to 383, ...) at most 144 rows name the same one
- capacity: int32 [4], replicated, may hold values from 72 to 144, as said below
- w_gate: bfloat16 [4096, 57344], P(None, 'dp'), may hold values from -0.09375 to 0.09375
- w_up: bfloat16 [4096, 57344], P(None, 'dp'), may hold values from -0.09375 to 0.09375
- w_down: bfloat16 [4096, 57344], P(None, 'dp'), may hold values from -0.046875 to 0.046875
Outputs:
- grad_tokens: bfloat16 [384, 4096], P('expert', 'dp')
- grad_probs: bfloat16 [384, 2], P('expert')
- grad_gate: bfloat16 [4096, 57344], P('expert', 'dp')
- grad_up: bfloat16 [4096, 57344], P('expert', 'dp')
- grad_down: bfloat16 [4096, 57344], P('expert', 'dp')
The draws below stay inside these ranges and needn't reach their ends.
Inputs may be any that keep to these rules, and one draw needn't show every extreme that they name: `expert_ids`: the two experts of a token differ. Among the 192 tokens of one group no expert is named more than 144 times, a bound that some block reaches. Some expert has capacity 144 and another one 144 // 2.
All inputs are finite; a program needn't handle non-finite values.
Results may differ from the reference program's by a relative error of at most 0.013.
Values may be sent and summed in bfloat16 or wider, within the bound.
No kernel may reach another device: no remote copies, remote signals or barrier semaphores. Data moves between devices by JAX's collectives and lax.ppermute only.
A program may use at most 256 MiB of HBM per device.

```python
import math
import jax
import jax.numpy as jnp
import numpy as np
from jax import lax

D = 4096
FF = 14336
EXPERTS = 4
TOK_GRP = 192
CAP = 144
HID_ALL = 57344
TOKENS = 384


def draw_capacity(key, part):
    key = jax.random.fold_in(key, 7)
    first_key, second_key = jax.random.split(key)
    values = jax.random.randint(first_key, (EXPERTS,), CAP // 2, CAP + 1, dtype=jnp.int32)
    order = jax.random.permutation(second_key, EXPERTS)
    values = values.at[order[0]].set(CAP)
    values = values.at[order[1]].set(CAP // 2)
    return values


def levels(own_key, extent, shards, least, high):
    factor_of, own = 1.0, jax.random.fold_in(own_key, 6)
    for dim, blocks in shards:
        heights = jnp.exp(jax.random.uniform(jax.random.fold_in(own, dim), (blocks,), jnp.float32, least / len(shards), high / len(shards)))
        factor_of = factor_of * jnp.repeat(heights, extent[dim] // blocks).reshape([-1 if axis == dim else 1 for axis in range(len(extent))])
    return factor_of


def deal_out(own_key, own, number, rows, number_of, top, reach, slope):
    sequence = jax.random.permutation(own_key, number_of)
    heavy_load, ordinary = load_shares(number_of, rows * top, reach, slope, True), load_shares(number_of, rows * top, reach, slope, False)
    places = jnp.arange(number_of)

    def named(sizes, offset_by):
        used = int((sizes > 0).sum())
        fixed = max(1, used // 4)
        passed = fixed + (places - fixed + offset_by * (used - fixed)) % max(1, number_of - fixed)
        return jnp.zeros((number_of,), jnp.int32).at[sequence[jnp.where(places < fixed, places, passed)]].set(jnp.asarray(sizes, jnp.int32))

    sizes = jnp.where(number % 4 == 0, named(heavy_load, number // 4), named(ordinary, number - number // 4 - 1))
    mixed = jax.random.permutation(jax.random.fold_in(own, 3), number_of)
    giver, taker = mixed[0:number_of // 2 * 2:2], mixed[1:number_of // 2 * 2:2]
    margin = jnp.minimum(sizes[giver] - 1, reach - sizes[taker]) // 2
    margin = jnp.where((giver == sequence[0]) | (taker == sequence[0]) | (sizes[taker] == 0), 0, jnp.maximum(margin, 0))
    passed = jax.random.randint(jax.random.fold_in(own, 4), (number_of // 2,), 0, 1 << 20) % (margin + 1)
    sizes = sizes.at[giver].add(-passed).at[taker].add(passed)
    items = jnp.searchsorted(jnp.cumsum(sizes), jnp.arange(rows * top), side="right").astype(jnp.int32)
    listing = items.reshape(top, rows).T
    listing = listing[jax.random.permutation(jax.random.fold_in(own, 1), rows)]
    offset_by = jax.random.randint(jax.random.fold_in(own, 2), (rows, 1), 0, top)
    return jnp.take_along_axis(listing, (jnp.arange(top)[None, :] + offset_by) % top, axis=1)


def load_shares(number_of, total, bound, skew, full):
    weights = [(1 << 20) // math.isqrt(standing ** skew) + 1 for standing in range(1, number_of + 1)]
    largest = bound if full else min(bound, max(-(-total // number_of), total * weights[0] // sum(weights)))
    least = 1 if total - largest >= number_of - 1 else 0
    given, surplus = [largest] + [least] * (number_of - 1), total - largest - least * (number_of - 1)
    while surplus > 0:
        candidates = [i for i in range(1, number_of) if given[i] < largest] or [i for i in range(1, number_of) if given[i] < bound]
        whole, left = sum([weights[i] for i in candidates]), surplus
        for i in candidates:
            more = min(bound - given[i], max(1, left * weights[i] // whole), surplus)
            given[i] = given[i] + more
            surplus = surplus - more
    return np.array(given)


def scatter_about(own_key, extent, width, reach, shards=(), held_as=jnp.bfloat16):
    values = jax.random.normal(own_key, extent, jnp.float32) * width
    if len(shards) > 0:
        values = levels(own_key, extent, shards, -0.22, 0.18) * values
    return jnp.clip(values, min=-reach, max=reach).astype(held_as)


def setup_inputs(seed: int = 0) -> dict:
    key_list = jax.random.split(jax.random.key(seed), 9)
    tokens = scatter_about(key_list[0], (TOKENS, D), 1.0, 6.0, ((0, 2),))
    grad_out = scatter_about(key_list[1], (TOKENS, D), 0.5, 3.0, ((0, 2),))
    gate_probs = jnp.clip(0.19921875 + 0.80078125 * jax.random.uniform(key_list[2], (TOKENS, 2), jnp.float32) ** levels(key_list[2], (TOKENS, 2), ((0, 2),), -0.2, 0.2), 0.19921875, 1.0).astype(jnp.bfloat16)
    expert_ids_keys = jax.random.split(jax.random.fold_in(key_list[3], 1), TOKENS // TOK_GRP)
    expert_ids_turns = jax.random.permutation(jax.random.fold_in(key_list[3], 3), TOKENS // TOK_GRP)
    expert_ids = jax.vmap(lambda own, number: deal_out(jax.random.fold_in(key_list[3], 2), own, number, TOK_GRP, EXPERTS, 2, CAP, 2))(expert_ids_keys, expert_ids_turns).reshape((TOKENS, 2))
    capacity = draw_capacity(jax.random.fold_in(key_list[8], 71), 0)
    w_gate = scatter_about(key_list[5], (D, HID_ALL), D ** -0.5, 0.09375, ((1, 16),))
    w_up = scatter_about(key_list[6], (D, HID_ALL), D ** -0.5, 0.09375, ((1, 16),))
    w_down = scatter_about(key_list[7], (D, HID_ALL), FF ** -0.5, 0.046875, ((1, 16),))
    return dict(tokens=tokens, grad_out=grad_out, gate_probs=gate_probs, expert_ids=expert_ids, capacity=capacity, w_gate=w_gate, w_up=w_up, w_down=w_down)


def routing_table(routes, capacity):
    flat_ids = routes.reshape(-1).astype(jnp.int32)
    expert_row = jnp.arange(EXPERTS, dtype=jnp.int32)
    onehot = (flat_ids[:, None] == expert_row[None, :]).astype(jnp.int32)
    earlier = jnp.cumsum(onehot, axis=0, dtype=jnp.int32) - onehot
    position = jnp.sum(earlier * onehot, axis=1, dtype=jnp.int32)
    limits = jnp.sum(onehot * capacity[None, :].astype(jnp.int32), axis=1, dtype=jnp.int32)
    target = flat_ids * CAP + position
    slot_rows = jnp.arange(EXPERTS * CAP, dtype=jnp.int32)
    chosen = (slot_rows[:, None] == target[None, :]) & (position < limits)[None, :]
    return chosen.astype(jnp.float32)


def expert_backward(rows_x, rows_u, rows_p, gate_weight, up_weight, down_weight):
    pre_gate = jnp.dot(rows_x, gate_weight, preferred_element_type=jnp.float32)
    pre_up = jnp.dot(rows_x, up_weight, preferred_element_type=jnp.float32)
    back_hidden = jnp.dot(rows_u, down_weight, preferred_element_type=jnp.float32)
    sigmoid_gate = jax.nn.sigmoid(pre_gate)
    activated = pre_gate * sigmoid_gate
    hidden = (activated * pre_up).astype(jnp.bfloat16)
    prob_rows = jnp.sum(hidden.astype(jnp.float32) * back_hidden, axis=1).astype(jnp.bfloat16)
    weight_col = rows_p.astype(jnp.float32)[:, None]
    scaled_back = weight_col * back_hidden
    d_gate = (scaled_back * pre_up * sigmoid_gate * (1.0 + pre_gate * (1.0 - sigmoid_gate))).astype(jnp.bfloat16)
    d_up = (scaled_back * activated).astype(jnp.bfloat16)
    scaled = (weight_col * rows_u.astype(jnp.float32)).astype(jnp.bfloat16)
    contract_rows = (((0,), (0,)), ((), ()))
    grad_gate = lax.dot_general(rows_x, d_gate, contract_rows, preferred_element_type=jnp.float32).astype(jnp.bfloat16)
    grad_up = lax.dot_general(rows_x, d_up, contract_rows, preferred_element_type=jnp.float32).astype(jnp.bfloat16)
    grad_down = lax.dot_general(scaled, hidden, contract_rows, preferred_element_type=jnp.float32).astype(jnp.bfloat16)
    contract_last = (((1,), (1,)), ((), ()))
    dx_rows = lax.dot_general(d_gate, gate_weight, contract_last, preferred_element_type=jnp.float32)
    dx_rows = dx_rows + lax.dot_general(d_up, up_weight, contract_last, preferred_element_type=jnp.float32)
    return dx_rows, prob_rows, grad_gate, grad_up, grad_down


def reference(tokens, grad_out, gate_probs, expert_ids, capacity, w_gate, w_up, w_down):
    groups = TOKENS // TOK_GRP
    pair_tables, merged_tables, slot_x, slot_u, slot_p = [], [], [], [], []
    for group_index in range(groups):
        first_row = group_index * TOK_GRP
        last_row = first_row + TOK_GRP
        chosen = routing_table(expert_ids[first_row:last_row], capacity)
        pair_table = chosen.reshape(EXPERTS * CAP, TOK_GRP, 2)
        merged = jnp.sum(pair_table, axis=2).astype(jnp.bfloat16)
        pair_tables.append(pair_table)
        merged_tables.append(merged)
        slot_x.append(jnp.dot(merged, tokens[first_row:last_row], preferred_element_type=jnp.float32).astype(jnp.bfloat16).reshape(EXPERTS, CAP, D))
        slot_u.append(jnp.dot(merged, grad_out[first_row:last_row], preferred_element_type=jnp.float32).astype(jnp.bfloat16).reshape(EXPERTS, CAP, D))
        weights_flat = gate_probs[first_row:last_row].reshape(-1).astype(jnp.float32)
        slot_p.append(jnp.dot(chosen, weights_flat, precision=lax.Precision.HIGHEST).astype(jnp.bfloat16).reshape(EXPERTS, CAP))
    stacked_x = jnp.stack(slot_x, axis=1)
    stacked_u = jnp.stack(slot_u, axis=1)
    stacked_p = jnp.stack(slot_p, axis=1)
    dx_list, prob_list, gate_list, up_list, down_list = [], [], [], [], []
    for expert_index in range(EXPERTS):
        first_col = expert_index * FF
        results = expert_backward(
            stacked_x[expert_index].reshape(groups * CAP, D),
            stacked_u[expert_index].reshape(groups * CAP, D),
            stacked_p[expert_index].reshape(groups * CAP),
            w_gate[:, first_col:first_col + FF], w_up[:, first_col:first_col + FF], w_down[:, first_col:first_col + FF])
        dx_list.append(results[0].reshape(groups, CAP, D))
        prob_list.append(results[1].reshape(groups, CAP))
        gate_list.append(results[2])
        up_list.append(results[3])
        down_list.append(results[4])
    dx_all = jnp.stack(dx_list, axis=0)
    prob_all = jnp.stack(prob_list, axis=0)
    token_parts, prob_parts = [], []
    for group_index in range(groups):
        returned = dx_all[:, group_index].reshape(EXPERTS * CAP, D)
        table = merged_tables[group_index].astype(jnp.float32)
        token_parts.append(jnp.dot(table.T, returned, precision=lax.Precision.HIGHEST).astype(jnp.bfloat16))
        returned_prob = prob_all[:, group_index].reshape(EXPERTS * CAP).astype(jnp.float32)
        prob_parts.append(jnp.einsum("rtk,r->tk", pair_tables[group_index], returned_prob, precision=lax.Precision.HIGHEST).astype(jnp.bfloat16))
    grad_tokens = jnp.concatenate(token_parts, axis=0)
    grad_probs = jnp.concatenate(prob_parts, axis=0)
    return grad_tokens, grad_probs, jnp.concatenate(gate_list, 1), jnp.concatenate(up_list, 1), jnp.concatenate(down_list, 1)
```

```python
import functools

import jax
import jax.numpy as jnp
from jax import lax
from jax.experimental import pallas as pl
from jax.experimental.pallas import tpu as pltpu
from jax.sharding import PartitionSpec as P

EXPERTS = 4
CAP = 144
SHORT = 256
EXTRA = 16
BF = jnp.bfloat16
F32 = jnp.float32
VMEM_LIMIT = 60 * 1024 * 1024

FIRST = (((0,), (0,)), ((), ()))
LAST = (((1,), (1,)), ((), ()))


def dot(a, b):
    return jnp.dot(a, b, preferred_element_type=F32)


def dotg(a, b, dims):
    return lax.dot_general(a, b, dims, preferred_element_type=F32)


def whole(shape):
    return pl.BlockSpec(shape, lambda *_: (0,) * len(shape), pipeline_mode=pl.Buffered(1))


def params():
    return pltpu.CompilerParams(vmem_limit_bytes=VMEM_LIMIT)


def whole_smem():
    return pl.BlockSpec(memory_space=pltpu.SMEM)


def in_place():
    return pl.BlockSpec(memory_space=pl.ANY)


def slot_table(routes, owner, limit, backwards):
    count = routes.shape[1]
    hit = (routes[:2] == owner.astype(F32)).astype(F32)
    named = jnp.sum(hit, axis=0, keepdims=True)
    weight = jnp.sum(hit * routes[2:4], axis=0, keepdims=True)
    row = lax.broadcasted_iota(jnp.int32, (count, count), 0)
    col = lax.broadcasted_iota(jnp.int32, (count, count), 1)
    earlier = (row < col).astype(F32).astype(BF)
    wide = jnp.broadcast_to(named, (16, count)).astype(BF)
    rank = dot(wide, earlier)[:1].astype(jnp.int32)
    kept = (named > 0) & (rank < limit)
    slot = lax.broadcasted_iota(jnp.int32, (CAP, count), 0)
    if backwards:
        slot = CAP - 1 - slot
    table = ((slot == rank) & kept).astype(F32)
    return table, jnp.sum(table * weight, axis=1, keepdims=True)


class Stream:
    def __init__(self, sources, slots, sems, block):
        self.sources, self.slots, self.sems, self.block = sources, slots, sems, block
        self.steps = sources[0].shape[1] // block

    def copy(self, i, step):
        source = self.sources[i]
        if self.steps > 1:
            source = source.at[:, pl.ds(pl.multiple_of(step * self.block, self.block), self.block)]
        slot = lax.rem(step, 2)
        return pltpu.make_async_copy(source, self.slots[i].at[slot], self.sems.at[i, slot])

    def first(self):
        for i in range(len(self.sources)):
            self.copy(i, 0).start()

    def ahead(self, step):
        @pl.when(step + 1 < self.steps)
        def _():
            for i in range(len(self.sources)):
                self.copy(i, step + 1).start()

    def wait(self, i, step):
        self.copy(i, step).wait()
        return self.slots[i].at[lax.rem(step, 2)]


def derivatives(x_ref, u_ref, p, stream, step):
    x = x_ref[...]
    wg = stream.wait(0, step)
    pre_gate = dot(x, wg[...])
    wu = stream.wait(1, step)
    pre_up = dot(x, wu[...])
    wd = stream.wait(2, step)
    back = dot(u_ref[...], wd[...])
    s = jax.nn.sigmoid(pre_gate)
    activated = pre_gate * s
    hidden = (activated * pre_up).astype(BF)
    scaled_back = p * back
    d_gate = (scaled_back * pre_up * s * (1.0 + pre_gate * (1.0 - s))).astype(BF)
    d_up = (scaled_back * activated).astype(BF)
    return d_gate, d_up, hidden, back, wg, wu


def pieces_of(total, size):
    return [(a, min(size, total - a)) for a in range(0, total, size)]


def own_body(packed, place_ref, cap_ref, routes_ref, tok_hbm, out_hbm, wg_hbm, wu_hbm, wd_hbm,
             dg_ref, du_ref, h_ref, part_ref, prob_ref, xq_ref, sq_ref, filled_ref,
             tok_ref, out_ref, x_ref, u_ref, p_ref, table_ref, acc_ref, wg_ref, wu_ref, wd_ref, sems, row_sems):
    step = pl.program_id(0)
    width, block = wg_ref.shape[1:]
    quarter = xq_ref.shape[1]
    stream = Stream((wg_hbm, wu_hbm, wd_hbm), (wg_ref, wu_ref, wd_ref), sems, block)
    owner, group = place_ref[0], place_ref[2]

    @pl.when(step == 0)
    def _():
        rows = [pltpu.make_async_copy(tok_hbm, tok_ref, row_sems.at[0]),
                pltpu.make_async_copy(out_hbm, out_ref, row_sems.at[1])]
        for copy in rows:
            copy.start()
        stream.first()
        table, p = slot_table(routes_ref[...].astype(F32), owner, cap_ref[owner], False)
        table_ref[...] = table.astype(BF)
        p_ref[...] = p
        filled_ref[...] = jnp.sum(table, axis=1, keepdims=True)
        acc_ref[...] = jnp.zeros_like(acc_ref)
        prob_ref[...] = jnp.zeros_like(prob_ref)
        rows[0].wait()
        x_ref[...] = dot(table_ref[...], tok_ref[...]).astype(BF)
        rows[1].wait()
        u_ref[...] = dot(table_ref[...], out_ref[...]).astype(BF)
        at = pl.ds(pl.multiple_of(group * quarter, quarter), quarter)
        xq_ref[...] = x_ref[:, at]
        sq_ref[...] = (p * u_ref[:, at].astype(F32)).astype(BF)

    stream.ahead(step)
    d_gate, d_up, hidden, back, wg, wu = derivatives(x_ref, u_ref, p_ref[...], stream, step)
    dg_ref[...] = d_gate
    du_ref[...] = d_up
    h_ref[...] = hidden
    prob_ref[...] += jnp.sum(hidden.astype(F32) * back, axis=1, keepdims=True)
    gate_t = d_gate.T
    up_t = d_up.T
    for a, n in pieces_of(width, 512):
        at = slice(a, a + n)
        acc_ref[at, :] += dot(wg[at, :], gate_t) + dot(wu[at, :], up_t)

    @pl.when(step == pl.num_programs(0) - 1)
    def _():
        table = table_ref[...]
        count = table.shape[1]
        shares, _, fw = part_ref.shape
        by_slot = (((0,), (1,)), ((), ()))
        for j in range(shares):
            part_ref[j, :count, :] = dotg(table, acc_ref[j * fw:(j + 1) * fw, :].astype(BF), by_slot).astype(BF)
        if packed:
            total = prob_ref[...]
            high = total.astype(BF).astype(F32)
            lane = lax.broadcasted_iota(jnp.int32, (CAP, 128), 1)
            both = jnp.where(lane == 0, high, jnp.where(lane == 1, total - high, 0.0)).astype(BF)
            by_token = dotg(both, table, FIRST)[:EXTRA].astype(BF)
            for j in range(shares):
                part_ref[j, count:, :] = jnp.zeros((EXTRA, fw), BF)
                part_ref[j, count:, :count] = by_token


def weight_slots(width, block):
    return [pltpu.VMEM((2, width, block), BF)] * 3 + [pltpu.SemaphoreType.DMA((3, 2))]


def own_group(place, capacity, routes, tokens, grad_out, wg, wu, wd, shares, groups, packed, block):
    count, width = tokens.shape
    hidden = wg.shape[1]
    tall = count + (EXTRA if packed else 0)
    fw = width // shares
    quarter = width // groups
    act = pl.BlockSpec((CAP, block), lambda j: (0, j))
    acts = jax.ShapeDtypeStruct((CAP, hidden), BF)
    column = jax.ShapeDtypeStruct((CAP, 1), F32)
    share = jax.ShapeDtypeStruct((CAP, quarter), BF)
    part = jax.ShapeDtypeStruct((shares, tall, fw), BF)
    rows = pltpu.VMEM((CAP, width), BF)
    tall_rows = pltpu.VMEM((count, width), BF)
    return pl.pallas_call(
        functools.partial(own_body, packed),
        grid=(hidden // block,),
        in_specs=[whole_smem(), whole_smem(), whole(routes.shape)] + [in_place()] * 5,
        out_specs=[act, act, act, whole(part.shape), whole(column.shape), whole(share.shape), whole(share.shape),
                   whole(column.shape)],
        out_shape=[acts, acts, acts, part, column, share, share, column],
        scratch_shapes=[tall_rows, tall_rows, rows, rows, pltpu.VMEM((CAP, 1), F32), pltpu.VMEM((CAP, count), BF),
                        pltpu.VMEM((width, CAP), F32)] + weight_slots(width, block) + [pltpu.SemaphoreType.DMA((2,))],
        compiler_params=params(),
        cost_estimate=pl.CostEstimate(
            flops=10 * CAP * width * hidden, bytes_accessed=6 * width * hidden, transcendentals=CAP * hidden),
        name="own_group",
    )(place, capacity, routes, tokens, grad_out, wg, wu, wd)


def weights_body(groups, place_ref, cap_ref, xq_ref, sq_ref, filled_ref, one_hbm, two_hbm, dg_ref, du_ref, h_ref,
                 wg_hbm, wu_hbm, wd_hbm, gg_ref, gu_ref, gd_ref,
                 one_ref, two_ref, xo_ref, uo_ref, po_ref, xs_ref, ss_ref, short_ref, wg_ref, wu_ref, wd_ref, sems, row_sems):
    step = pl.program_id(0)
    owner, parity, group = place_ref[0], place_ref[1], place_ref[2]
    quarter = xs_ref.shape[1]
    others = xo_ref.shape[0]
    count = one_ref.shape[1] - EXTRA
    lead = SHORT - CAP
    shared = CAP - lead
    stream = Stream((wg_hbm, wu_hbm, wd_hbm), (wg_ref, wu_ref, wd_ref), sems, wg_ref.shape[2])

    def joined(mine, other):
        return jnp.concatenate([mine, other], axis=0)

    def merged(mine, other):
        return jnp.concatenate([mine[:lead], mine[lead:] + other[:shared], other[shared:]], axis=0)

    @pl.when(step == 0)
    def _():
        rows = [pltpu.make_async_copy(one_hbm, one_ref, row_sems.at[0]),
                pltpu.make_async_copy(two_hbm, two_ref, row_sems.at[1])]
        for copy in rows:
            copy.start()
        stream.first()
        for copy in rows:
            copy.wait()
        filled = jnp.sum(filled_ref[...])
        for g in range(groups - 1):
            at = slice(g * CAP, (g + 1) * CAP)
            routes = one_ref[g, count:count + 8, :count].astype(F32)
            table, p = slot_table(routes, owner, cap_ref[owner], groups == 2)
            filled += jnp.sum(table)
            po_ref[at, :] = p
            table = table.astype(BF)
            from_one = dot(table, one_ref[g, :count, :]).astype(BF)
            from_two = dot(table, two_ref[g, :count, :]).astype(BF)

            @pl.when(parity == 0)
            def _():
                xo_ref[at, :] = from_one
                uo_ref[at, :] = from_two

            @pl.when(parity == 1)
            def _():
                xo_ref[at, :] = from_two
                uo_ref[at, :] = from_one

        fits = filled <= SHORT if groups == 2 else jnp.bool_(False)
        short_ref[0] = fits.astype(jnp.int32)
        part = pl.ds(pl.multiple_of(group * quarter, quarter), quarter)
        mine, scaled = xq_ref[...], sq_ref[...]
        other = xo_ref[:, part]
        scaled_other = (po_ref[...] * uo_ref[:, part].astype(F32)).astype(BF)
        if groups == 2:
            @pl.when(fits)
            def _():
                xs_ref[:SHORT, :] = merged(mine, other)
                ss_ref[:SHORT, :] = merged(scaled, scaled_other)

        @pl.when(jnp.logical_not(fits))
        def _():
            xs_ref[...] = joined(mine, other)
            ss_ref[...] = joined(scaled, scaled_other)

    stream.ahead(step)
    d_gate, d_up, hidden, _, _, _ = derivatives(xo_ref, uo_ref, po_ref[...], stream, step)

    def grads(join, rows):
        xs = xs_ref[:rows, :]
        gg_ref[...] = dotg(xs, join(dg_ref[...], d_gate), FIRST).astype(BF)
        gu_ref[...] = dotg(xs, join(du_ref[...], d_up), FIRST).astype(BF)
        gd_ref[...] = dotg(ss_ref[:rows, :], join(h_ref[...], hidden), FIRST).astype(BF)

    if groups == 2:
        @pl.when(short_ref[0] == 1)
        def _():
            grads(merged, SHORT)

    @pl.when(short_ref[0] == 0)
    def _():
        grads(joined, CAP + others)


def weight_grads(place, capacity, xq, sq, filled, one, two, dg, du, h, wg, wu, wd, groups, block):
    width, hidden = wg.shape
    others = (groups - 1) * CAP
    quarter = width // groups
    act = pl.BlockSpec((CAP, block), lambda j: (0, j))
    grad = pl.BlockSpec((quarter, block), lambda j: (0, j))
    arrived = pltpu.VMEM(one.shape, BF)
    rows = pltpu.VMEM((others, width), BF)
    share = pltpu.VMEM((CAP + others, quarter), BF)
    return pl.pallas_call(
        functools.partial(weights_body, groups),
        grid=(hidden // block,),
        in_specs=[whole_smem(), whole_smem(), whole(xq.shape), whole(sq.shape), whole(filled.shape), in_place(), in_place(),
                  act, act, act, in_place(), in_place(), in_place()],
        out_specs=[grad] * 3,
        out_shape=[jax.ShapeDtypeStruct((quarter, hidden), BF)] * 3,
        scratch_shapes=[arrived, arrived, rows, rows, pltpu.VMEM((others, 1), F32), share, share,
                        pltpu.SMEM((1,), jnp.int32)] + weight_slots(width, block) + [pltpu.SemaphoreType.DMA((2,))],
        compiler_params=params(),
        cost_estimate=pl.CostEstimate(
            flops=6 * others * width * hidden + 6 * (CAP + others) * quarter * hidden,
            bytes_accessed=6 * width * hidden + 6 * quarter * hidden, transcendentals=others * hidden),
        name="weight_grads",
    )(place, capacity, xq, sq, filled, one, two, dg, du, h, wg, wu, wd)


def block_of(hidden, largest):
    for size in (512, 256, 128):
        if size <= largest and hidden % size == 0:
            return size
    return hidden


def per_device(tokens, grad_out, gate_probs, expert_ids, capacity, w_gate, w_up, w_down):
    groups = lax.axis_size("expert")
    shares = lax.axis_size("dp")
    count, width = tokens.shape
    hidden = w_gate.shape[1]
    per_expert = shares // EXPERTS
    index = lax.axis_index("dp")
    owner = index // per_expert
    parity = index % 2
    place = jnp.stack([owner, parity, lax.axis_index("expert")]).astype(jnp.int32)
    packed = width // shares >= count

    routes = jnp.concatenate([expert_ids.T.astype(BF), gate_probs.T, jnp.zeros((EXTRA - 4, count), BF)], axis=0)
    send = jnp.concatenate(
        [jnp.where(parity == 0, tokens, grad_out), jnp.pad(routes, ((0, 0), (0, width - count)))], axis=0)
    arounds = [[(i, (i + shift) % groups) for i in range(groups)] for shift in range(1, groups)]
    one = [lax.ppermute(send, "expert", around) for around in arounds]

    dg, du, h, part, prob, xq, sq, filled = own_group(
        place, capacity, routes, tokens, grad_out, w_gate, w_up, w_down, shares, groups, packed, block_of(hidden, 512))

    one, part = lax.optimization_barrier((one, part))
    swap = [(i, i ^ 1) for i in range(shares)]
    two = [lax.ppermute(rows, "dp", swap) for rows in one]
    arrived = lax.all_to_all(part, "dp", split_axis=0, concat_axis=0, tiled=True)

    def stacked(parts):
        return parts[0][None] if len(parts) == 1 else jnp.stack(parts)

    grad_gate, grad_up, grad_down = weight_grads(
        place, capacity, xq, sq, filled, stacked(one), stacked(two), dg, du, h, w_gate, w_up, w_down, groups,
        block_of(hidden, 512))

    token_grad = jnp.sum(arrived[:, :count].astype(F32), axis=0).astype(BF)
    if packed:
        ends = arrived[:, count:count + 2, :count].astype(F32)
        by_expert = jnp.sum(ends.reshape(EXPERTS, per_expert * 2, count), axis=1)
    else:
        table, _ = slot_table(routes.astype(F32), owner, capacity[owner], False)
        mine = jnp.sum(table * prob, axis=0)
        one_hot = (jnp.arange(EXPERTS) == owner).astype(F32)
        by_expert = lax.psum(one_hot[:, None] * mine[None, :], "dp")
    match = expert_ids[:, :, None] == jnp.arange(EXPERTS, dtype=jnp.int32)
    prob_grad = jnp.sum(jnp.where(match, by_expert.T[:, None, :], 0.0), axis=2).astype(BF)
    return (token_grad, prob_grad, grad_gate, grad_up, grad_down)


def solution(mesh):
    return jax.shard_map(
        per_device,
        mesh=mesh,
        in_specs=(
            P("expert", None),
            P("expert", None),
            P("expert", None),
            P("expert", None),
            P(),
            P(None, "dp"),
            P(None, "dp"),
            P(None, "dp"),
        ),
        out_specs=(
            P("expert", "dp"),
            P("expert", None),
            P("expert", "dp"),
            P("expert", "dp"),
            P("expert", "dp"),
        ),
        check_vma=False,
    )
```

```python
import functools

import jax
import jax.numpy as jnp
from jax import lax
from jax.experimental import pallas as pl
from jax.experimental.pallas import tpu as pltpu
from jax.sharding import PartitionSpec as P

EXPERTS = 4
CAP = 144
SHORT = 256
EXTRA = 16
BF = jnp.bfloat16
F32 = jnp.float32
VMEM_LIMIT = 60 * 1024 * 1024

FIRST = (((0,), (0,)), ((), ()))
LAST = (((1,), (1,)), ((), ()))


def dot(a, b):
    return jnp.dot(a, b, preferred_element_type=F32)


def dotg(a, b, dims):
    return lax.dot_general(a, b, dims, preferred_element_type=F32)


def whole(shape):
    return pl.BlockSpec(shape, lambda *_: (0,) * len(shape), pipeline_mode=pl.Buffered(1))


def params():
    return pltpu.CompilerParams(vmem_limit_bytes=VMEM_LIMIT)


def whole_smem():
    return pl.BlockSpec(memory_space=pltpu.SMEM)


def in_place():
    return pl.BlockSpec(memory_space=pl.ANY)


def my_place(shares):
    index = lax.axis_index("dp")
    return index // (shares // EXPERTS), index % 2, lax.axis_index("expert")


def pack_body(shares, ids_ref, probs_ref, tok_hbm, out_hbm, routes_ref, send_hbm, tail_ref, sems):
    _, parity, _ = my_place(shares)
    count = tok_hbm.shape[0]
    top = send_hbm.at[:count]

    @pl.when(parity == 0)
    def _():
        pltpu.make_async_copy(tok_hbm, top, sems.at[0]).start()

    @pl.when(parity == 1)
    def _():
        pltpu.make_async_copy(out_hbm, top, sems.at[0]).start()

    ids = ids_ref[...].astype(F32)
    routes = jnp.concatenate([ids, probs_ref[...].astype(F32), jnp.zeros((EXTRA - 4, count), F32)], axis=0).astype(BF)
    routes_ref[...] = routes
    tail_ref[...] = jnp.zeros_like(tail_ref)
    tail_ref[:, :count] = routes
    below = pltpu.make_async_copy(tail_ref, send_hbm.at[pl.ds(count, EXTRA)], sems.at[1])
    below.start()
    below.wait()
    pltpu.make_async_copy(tok_hbm, top, sems.at[0]).wait()


def pack(ids, probs, tokens, grad_out, shares):
    count, width = tokens.shape
    return pl.pallas_call(
        functools.partial(pack_body, shares),
        in_specs=[whole(ids.shape), whole(probs.shape), in_place(), in_place()],
        out_specs=[whole((EXTRA, count)), in_place()],
        out_shape=[jax.ShapeDtypeStruct((EXTRA, count), BF), jax.ShapeDtypeStruct((count + EXTRA, width), BF)],
        scratch_shapes=[pltpu.VMEM((EXTRA, width), BF), pltpu.SemaphoreType.DMA((2,))],
        cost_estimate=pl.CostEstimate(flops=0, bytes_accessed=4 * count * width, transcendentals=0),
        name="pack",
    )(ids, probs, tokens, grad_out)


def slot_table(routes, owner, limit, backwards):
    count = routes.shape[1]
    hit = (routes[:2] == owner.astype(F32)).astype(F32)
    named = jnp.sum(hit, axis=0, keepdims=True)
    weight = jnp.sum(hit * routes[2:4], axis=0, keepdims=True)
    row = lax.broadcasted_iota(jnp.int32, (count, count), 0)
    col = lax.broadcasted_iota(jnp.int32, (count, count), 1)
    earlier = (row < col).astype(F32).astype(BF)
    wide = jnp.broadcast_to(named, (16, count)).astype(BF)
    rank = dot(wide, earlier)[:1].astype(jnp.int32)
    kept = (named > 0) & (rank < limit)
    slot = lax.broadcasted_iota(jnp.int32, (CAP, count), 0)
    slot = jnp.where(backwards, CAP - 1 - slot, slot)
    table = ((slot == rank) & kept).astype(F32)
    return table, jnp.sum(table * weight, axis=1, keepdims=True)


class Stream:
    def __init__(self, sources, slots, sems, block, steps):
        self.sources, self.slots, self.sems, self.block = sources, slots, sems, block
        self.steps, self.whole = steps, sources[0].shape[1] == block

    def copy(self, i, step):
        source = self.sources[i]
        if not self.whole:
            source = source.at[:, pl.ds(pl.multiple_of(step * self.block, self.block), self.block)]
        slot = lax.rem(step, 2)
        return pltpu.make_async_copy(source, self.slots[i].at[slot], self.sems.at[i, slot])

    def first(self):
        for i in range(len(self.sources)):
            self.copy(i, 0).start()

    def ahead(self, step):
        @pl.when(step + 1 < self.steps)
        def _():
            for i in range(len(self.sources)):
                self.copy(i, step + 1).start()

    def wait(self, i, step):
        self.copy(i, step).wait()
        return self.slots[i].at[lax.rem(step, 2)]


def derivatives(x_ref, u_ref, p, stream, step):
    x = x_ref[...]
    wg = stream.wait(0, step)
    pre_gate = dot(x, wg[...])
    wu = stream.wait(1, step)
    pre_up = dot(x, wu[...])
    wd = stream.wait(2, step)
    back = dot(u_ref[...], wd[...])
    s = jax.nn.sigmoid(pre_gate)
    activated = pre_gate * s
    hidden = (activated * pre_up).astype(BF)
    scaled_back = p * back
    d_gate = (scaled_back * pre_up * s * (1.0 + pre_gate * (1.0 - s))).astype(BF)
    d_up = (scaled_back * activated).astype(BF)
    return d_gate, d_up, hidden, back, wg, wu


def pieces_of(total, size):
    return [(a, min(size, total - a)) for a in range(0, total, size)]


def own_body(packed, early, groups, cap_ref, routes_ref, tok_hbm, out_hbm, wg_hbm, wu_hbm, wd_hbm, *refs):
    acts_refs, refs = (refs[:3], refs[3:]) if early is None else (refs[:4], refs[4:])
    (part_ref, prob_ref, xq_ref, sq_ref, filled_ref, tok_ref, out_ref, x_ref, u_ref, p_ref, table_ref, acc_ref,
     wg_ref, wu_ref, wd_ref, sems, row_sems) = refs
    step = pl.program_id(0)
    width, block = wg_ref.shape[1:]
    quarter = xq_ref.shape[1]
    stream = Stream((wg_hbm, wu_hbm, wd_hbm), (wg_ref, wu_ref, wd_ref), sems, block, wg_hbm.shape[1] // block)
    owner, _, group = my_place(part_ref.shape[0])

    @pl.when(step == 0)
    def _():
        rows = [pltpu.make_async_copy(tok_hbm, tok_ref, row_sems.at[0]),
                pltpu.make_async_copy(out_hbm, out_ref, row_sems.at[1])]
        for copy in rows:
            copy.start()
        stream.first()
        table, p = slot_table(routes_ref[...].astype(F32), owner, cap_ref[owner], (group == 1) & (groups == 2))
        table_ref[...] = table.astype(BF)
        p_ref[...] = p
        filled_ref[...] = jnp.sum(table, axis=1, keepdims=True)
        acc_ref[...] = jnp.zeros_like(acc_ref)
        prob_ref[...] = jnp.zeros_like(prob_ref)
        rows[0].wait()
        x_ref[...] = dot(table_ref[...], tok_ref[...]).astype(BF)
        rows[1].wait()
        u_ref[...] = dot(table_ref[...], out_ref[...]).astype(BF)
        at = pl.ds(pl.multiple_of(group * quarter, quarter), quarter)
        xq_ref[...] = x_ref[:, at]
        sq_ref[...] = (p * u_ref[:, at].astype(F32)).astype(BF)

    stream.ahead(step)
    d_gate, d_up, hidden, back, wg, wu = derivatives(x_ref, u_ref, p_ref[...], stream, step)
    acts = (d_gate, d_up, hidden)

    def store_early():
        for ref, value in zip(acts_refs, acts):
            ref[...] = value

    if early is None:
        store_early()
    else:
        pl.when(step < early)(store_early)

        @pl.when(step >= early)
        def _():
            for i, value in enumerate(acts):
                acts_refs[3][i] = value

    prob_ref[...] += jnp.sum(hidden.astype(F32) * back, axis=1, keepdims=True)
    gate_t = d_gate.T
    up_t = d_up.T
    for a, n in pieces_of(width, 512):
        at = slice(a, a + n)
        acc_ref[at, :] += dot(wg[at, :], gate_t) + dot(wu[at, :], up_t)

    @pl.when(step == pl.num_programs(0) - 1)
    def _():
        table = table_ref[...]
        count = table.shape[1]
        shares, _, fw = part_ref.shape
        by_slot = (((0,), (1,)), ((), ()))
        for j in range(shares):
            part_ref[j, :count, :] = dotg(table, acc_ref[j * fw:(j + 1) * fw, :].astype(BF), by_slot).astype(BF)
        if packed:
            total = prob_ref[...]
            high = total.astype(BF).astype(F32)
            lane = lax.broadcasted_iota(jnp.int32, (CAP, 128), 1)
            both = jnp.where(lane == 0, high, jnp.where(lane == 1, total - high, 0.0)).astype(BF)
            by_token = dotg(both, table, FIRST)[:EXTRA].astype(BF)
            for j in range(shares):
                part_ref[j, count:, :] = jnp.zeros((EXTRA, fw), BF)
                part_ref[j, count:, :count] = by_token


def weight_slots(width, block):
    return [pltpu.VMEM((2, width, block), BF)] * 3 + [pltpu.SemaphoreType.DMA((3, 2))]


def own_group(capacity, routes, tokens, grad_out, wg, wu, wd, shares, groups, packed, block, early):
    count, width = tokens.shape
    hidden = wg.shape[1]
    steps = hidden // block
    tall = count + (EXTRA if packed else 0)
    fw = width // shares
    quarter = width // groups
    act_specs = [pl.BlockSpec((CAP, block), lambda j: (0, jnp.minimum(j, early - 1)))] * 3
    acts = [jax.ShapeDtypeStruct((CAP, early * block), BF)] * 3
    if early < steps:
        act_specs.append(pl.BlockSpec((3, CAP, block), lambda j: (0, 0, jnp.maximum(j - early, 0))))
        acts.append(jax.ShapeDtypeStruct((3, CAP, (steps - early) * block), BF))
    column = jax.ShapeDtypeStruct((CAP, 1), F32)
    share = jax.ShapeDtypeStruct((CAP, quarter), BF)
    part = jax.ShapeDtypeStruct((shares, tall, fw), BF)
    rows = pltpu.VMEM((CAP, width), BF)
    tall_rows = pltpu.VMEM((count, width), BF)
    return pl.pallas_call(
        functools.partial(own_body, packed, early if early < steps else None, groups),
        grid=(steps,),
        in_specs=[whole_smem(), whole(routes.shape)] + [in_place()] * 5,
        out_specs=act_specs + [whole(part.shape), whole(column.shape), whole(share.shape), whole(share.shape),
                               whole(column.shape)],
        out_shape=acts + [part, column, share, share, column],
        scratch_shapes=[tall_rows, tall_rows, rows, rows, pltpu.VMEM((CAP, 1), F32), pltpu.VMEM((CAP, count), BF),
                        pltpu.VMEM((width, CAP), F32)] + weight_slots(width, block) + [pltpu.SemaphoreType.DMA((2,))],
        compiler_params=params(),
        cost_estimate=pl.CostEstimate(
            flops=10 * CAP * width * hidden, bytes_accessed=6 * width * hidden, transcendentals=CAP * hidden),
        name="own_group",
    )(capacity, routes, tokens, grad_out, wg, wu, wd)


def joined(mine, other):
    return jnp.concatenate([mine, other], axis=0)


def merged(group, mine, other):
    first, last = jnp.where(group == 0, mine, other), jnp.where(group == 0, other, mine)
    lead = SHORT - CAP
    shared = CAP - lead
    return jnp.concatenate([first[:lead], first[lead:] + last[:shared], last[shared:]], axis=0)


def store_grads(groups, group, fits_ref, xs_ref, ss_ref, mine, other, out_refs):
    def grads(join, rows):
        for i, (rows_ref, out_ref) in enumerate(zip((xs_ref, xs_ref, ss_ref), out_refs)):
            out_ref[...] = dotg(rows_ref[:rows, :], join(mine(i), other(i)), FIRST).astype(BF)

    if groups == 2:
        @pl.when(fits_ref[0] == 1)
        def _():
            grads(functools.partial(merged, group), SHORT)

    @pl.when(fits_ref[0] == 0)
    def _():
        grads(joined, xs_ref.shape[0])


def again_body(groups, shares, steps, cap_ref, xq_ref, sq_ref, filled_ref, one_hbm, two_hbm, dg_ref, du_ref, h_ref,
               wg_hbm, wu_hbm, wd_hbm, gg_ref, gu_ref, gd_ref, xs_ref, ss_ref, fits_ref,
               one_ref, two_ref, xo_ref, uo_ref, po_ref, wg_ref, wu_ref, wd_ref, sems, row_sems):
    step = pl.program_id(0)
    owner, parity, group = my_place(shares)
    quarter = xs_ref.shape[1]
    count = one_ref.shape[1] - EXTRA
    stream = Stream((wg_hbm, wu_hbm, wd_hbm), (wg_ref, wu_ref, wd_ref), sems, wg_ref.shape[2], steps)

    @pl.when(step == 0)
    def _():
        rows = [pltpu.make_async_copy(one_hbm, one_ref, row_sems.at[0]),
                pltpu.make_async_copy(two_hbm, two_ref, row_sems.at[1])]
        for copy in rows:
            copy.start()
        stream.first()
        for copy in rows:
            copy.wait()
        filled = jnp.sum(filled_ref[...])
        for g in range(groups - 1):
            at = slice(g * CAP, (g + 1) * CAP)
            routes = one_ref[g, count:count + 8, :count].astype(F32)
            table, p = slot_table(routes, owner, cap_ref[owner], (group == 0) & (groups == 2))
            filled += jnp.sum(table)
            po_ref[at, :] = p
            table = table.astype(BF)
            from_one = dot(table, one_ref[g, :count, :]).astype(BF)
            from_two = dot(table, two_ref[g, :count, :]).astype(BF)

            @pl.when(parity == 0)
            def _():
                xo_ref[at, :] = from_one
                uo_ref[at, :] = from_two

            @pl.when(parity == 1)
            def _():
                xo_ref[at, :] = from_two
                uo_ref[at, :] = from_one

        fits = filled <= SHORT if groups == 2 else jnp.bool_(False)
        fits_ref[0] = fits.astype(jnp.int32)
        part = pl.ds(pl.multiple_of(group * quarter, quarter), quarter)
        mine, scaled = xq_ref[...], sq_ref[...]
        other = xo_ref[:, part]
        scaled_other = (po_ref[...] * uo_ref[:, part].astype(F32)).astype(BF)
        if groups == 2:
            @pl.when(fits)
            def _():
                xs_ref[:SHORT, :] = merged(group, mine, other)
                ss_ref[:SHORT, :] = merged(group, scaled, scaled_other)

        @pl.when(jnp.logical_not(fits))
        def _():
            xs_ref[...] = joined(mine, other)
            ss_ref[...] = joined(scaled, scaled_other)

    stream.ahead(step)
    acts = derivatives(xo_ref, uo_ref, po_ref[...], stream, step)
    own = (dg_ref, du_ref, h_ref)
    store_grads(groups, group, fits_ref, xs_ref, ss_ref, lambda i: own[i][...], lambda i: acts[i], (gg_ref, gu_ref, gd_ref))


def grads_again(capacity, xq, sq, filled, one, two, dg, du, h, wg, wu, wd, groups, shares, block):
    width, hidden = wg.shape
    others = (groups - 1) * CAP
    quarter = width // groups
    steps = dg.shape[1] // block
    act = pl.BlockSpec((CAP, block), lambda j: (0, j))
    grad = pl.BlockSpec((quarter, block), lambda j: (0, j))
    arrived = pltpu.VMEM(one.shape, BF)
    rows = pltpu.VMEM((others, width), BF)
    joint = jax.ShapeDtypeStruct((CAP + others, quarter), BF)
    return pl.pallas_call(
        functools.partial(again_body, groups, shares, steps),
        grid=(steps,),
        in_specs=[whole_smem(), whole(xq.shape), whole(sq.shape), whole(filled.shape), in_place(), in_place(),
                  act, act, act, in_place(), in_place(), in_place()],
        out_specs=[grad] * 3 + [whole(joint.shape)] * 2 + [whole_smem()],
        out_shape=[jax.ShapeDtypeStruct((quarter, hidden), BF)] * 3 + [joint] * 2 + [jax.ShapeDtypeStruct((1,), jnp.int32)],
        scratch_shapes=[arrived, arrived, rows, rows, pltpu.VMEM((others, 1), F32)]
        + weight_slots(width, block) + [pltpu.SemaphoreType.DMA((2,))],
        compiler_params=params(),
        cost_estimate=pl.CostEstimate(
            flops=(6 * others * width + 6 * (CAP + others) * quarter) * steps * block,
            bytes_accessed=6 * (width + quarter) * steps * block, transcendentals=others * steps * block),
        name="grads_again",
    )(capacity, xq, sq, filled, one, two, dg, du, h, wg, wu, wd)


def given_body(groups, shares, fits_ref, xs_ref, ss_ref, mine_ref, other_ref, gg_in, gu_in, gd_in, gg_ref, gu_ref, gd_ref):
    _, _, group = my_place(shares)
    store_grads(groups, group, fits_ref, xs_ref, ss_ref, lambda i: mine_ref[i], lambda i: other_ref[i], (gg_ref, gu_ref, gd_ref))


def grads_given(fits, xs, ss, mine, other, grads, groups, shares, block):
    quarter, hidden = grads[0].shape
    steps = mine.shape[2] // block
    early = hidden // block - steps
    act = pl.BlockSpec((3, CAP, block), lambda j: (0, 0, j))
    grad = pl.BlockSpec((quarter, block), lambda j: (0, j + early))
    return pl.pallas_call(
        functools.partial(given_body, groups, shares),
        grid=(steps,),
        in_specs=[whole_smem(), whole(xs.shape), whole(ss.shape), act, act] + [in_place()] * 3,
        out_specs=[grad] * 3,
        out_shape=[jax.ShapeDtypeStruct((quarter, hidden), BF)] * 3,
        input_output_aliases={5: 0, 6: 1, 7: 2},
        compiler_params=params(),
        cost_estimate=pl.CostEstimate(
            flops=6 * xs.shape[0] * quarter * steps * block, bytes_accessed=6 * quarter * steps * block, transcendentals=0),
        name="grads_given",
    )(fits, xs, ss, mine, other, *grads)


def block_of(hidden, largest):
    for size in (512, 256, 128):
        if size <= largest and hidden % size == 0:
            return size
    return hidden


def per_device(tokens, grad_out, gate_probs, expert_ids, capacity, w_gate, w_up, w_down):
    groups = lax.axis_size("expert")
    shares = lax.axis_size("dp")
    count, width = tokens.shape
    hidden = w_gate.shape[1]
    per_expert = shares // EXPERTS
    packed = width // shares >= count
    block = block_of(hidden, 512)
    steps = hidden // block
    early = steps - steps * 3 // 7 if groups == 2 else steps

    routes, send = pack(expert_ids.T, gate_probs.T, tokens, grad_out, shares)
    arounds = [[(i, (i + shift) % groups) for i in range(groups)] for shift in range(1, groups)]
    one = [lax.ppermute(send, "expert", around) for around in arounds]

    *acts, part, prob, xq, sq, filled = own_group(
        capacity, routes, tokens, grad_out, w_gate, w_up, w_down, shares, groups, packed, block, early)

    one, part = lax.optimization_barrier((one, part))
    swap = [(i, i ^ 1) for i in range(shares)]
    two = [lax.ppermute(rows, "dp", swap) for rows in one]
    if early < steps:
        late = acts.pop()
        late_other = lax.ppermute(late, "expert", arounds[0])
    arrived = lax.all_to_all(part, "dp", split_axis=0, concat_axis=0, tiled=True)

    def stacked(parts):
        return parts[0][None] if len(parts) == 1 else jnp.stack(parts)

    *grads, xs, ss, fits = grads_again(
        capacity, xq, sq, filled, stacked(one), stacked(two), *acts, w_gate, w_up, w_down, groups, shares, block)
    if early < steps:
        grads = grads_given(fits, xs, ss, late, late_other, grads, groups, shares, block)
    grad_gate, grad_up, grad_down = grads

    token_grad = jnp.sum(arrived[:, :count].astype(F32), axis=0).astype(BF)
    if packed:
        ends = arrived[:, count:count + 2, :count].astype(F32)
        by_expert = jnp.sum(ends.reshape(EXPERTS, per_expert * 2, count), axis=1)
    else:
        owner, _, group = my_place(shares)
        table, _ = slot_table(routes.astype(F32), owner, capacity[owner], (group == 1) & (groups == 2))
        mine = jnp.sum(table * prob, axis=0)
        one_hot = (jnp.arange(EXPERTS) == owner).astype(F32)
        by_expert = lax.psum(one_hot[:, None] * mine[None, :], "dp")
    match = expert_ids[:, :, None] == jnp.arange(EXPERTS, dtype=jnp.int32)
    prob_grad = jnp.sum(jnp.where(match, by_expert.T[:, None, :], 0.0), axis=2).astype(BF)
    return (token_grad, prob_grad, grad_gate, grad_up, grad_down)


def solution(mesh):
    return jax.shard_map(
        per_device,
        mesh=mesh,
        in_specs=(
            P("expert", None),
            P("expert", None),
            P("expert", None),
            P("expert", None),
            P(),
            P(None, "dp"),
            P(None, "dp"),
            P(None, "dp"),
        ),
        out_specs=(
            P("expert", "dp"),
            P("expert", None),
            P("expert", "dp"),
            P("expert", "dp"),
            P("expert", "dp"),
        ),
        check_vma=False,
    )
```

```python
import functools

import jax
import jax.numpy as jnp
from jax import lax
from jax.experimental import pallas as pl
from jax.experimental.pallas import tpu as pltpu
from jax.sharding import PartitionSpec as P

EXPERTS = 4
CAP = 144
SHORT = 256
EXTRA = 16
BF = jnp.bfloat16
F32 = jnp.float32
VMEM_LIMIT = 60 * 1024 * 1024

FIRST = (((0,), (0,)), ((), ()))
LAST = (((1,), (1,)), ((), ()))


def dot(a, b):
    return jnp.dot(a, b, preferred_element_type=F32)


def dotg(a, b, dims):
    return lax.dot_general(a, b, dims, preferred_element_type=F32)


def whole(shape):
    return pl.BlockSpec(shape, lambda *_: (0,) * len(shape), pipeline_mode=pl.Buffered(1))


def params():
    return pltpu.CompilerParams(vmem_limit_bytes=VMEM_LIMIT)


def whole_smem():
    return pl.BlockSpec(memory_space=pltpu.SMEM)


def in_place():
    return pl.BlockSpec(memory_space=pl.ANY)


def my_place(shares):
    index = lax.axis_index("dp")
    return index // (shares // EXPERTS), index % 2, lax.axis_index("expert")


def pack_body(shares, ids_ref, probs_ref, tok_hbm, out_hbm, routes_ref, send_ref, sem):
    _, parity, _ = my_place(shares)
    count = tok_hbm.shape[0]
    top = send_ref.at[:count]

    @pl.when(parity == 0)
    def _():
        pltpu.make_async_copy(tok_hbm, top, sem).start()

    @pl.when(parity == 1)
    def _():
        pltpu.make_async_copy(out_hbm, top, sem).start()

    ids = ids_ref[...].astype(F32)
    routes = jnp.concatenate([ids, probs_ref[...].astype(F32), jnp.zeros((EXTRA - 4, count), F32)], axis=0).astype(BF)
    routes_ref[...] = routes
    send_ref[count:, :] = jnp.zeros((EXTRA, send_ref.shape[1]), BF)
    send_ref[count:, :count] = routes
    pltpu.make_async_copy(tok_hbm, top, sem).wait()


def pack(ids, probs, tokens, grad_out, shares):
    count, width = tokens.shape
    return pl.pallas_call(
        functools.partial(pack_body, shares),
        in_specs=[whole(ids.shape), whole(probs.shape), in_place(), in_place()],
        out_specs=[whole((EXTRA, count)), whole((count + EXTRA, width))],
        out_shape=[jax.ShapeDtypeStruct((EXTRA, count), BF), jax.ShapeDtypeStruct((count + EXTRA, width), BF)],
        scratch_shapes=[pltpu.SemaphoreType.DMA(())],
        compiler_params=params(),
        cost_estimate=pl.CostEstimate(flops=0, bytes_accessed=4 * count * width, transcendentals=0),
        name="pack",
    )(ids, probs, tokens, grad_out)


def slot_table(routes, owner, limit, backwards):
    count = routes.shape[1]
    hit = (routes[:2] == owner.astype(F32)).astype(F32)
    named = jnp.sum(hit, axis=0, keepdims=True)
    weight = jnp.sum(hit * routes[2:4], axis=0, keepdims=True)
    row = lax.broadcasted_iota(jnp.int32, (count, count), 0)
    col = lax.broadcasted_iota(jnp.int32, (count, count), 1)
    earlier = (row < col).astype(F32).astype(BF)
    wide = jnp.broadcast_to(named, (16, count)).astype(BF)
    rank = dot(wide, earlier)[:1].astype(jnp.int32)
    kept = (named > 0) & (rank < limit)
    slot = lax.broadcasted_iota(jnp.int32, (CAP, count), 0)
    slot = jnp.where(backwards, CAP - 1 - slot, slot)
    table = ((slot == rank) & kept).astype(F32)
    return table, jnp.sum(table * weight, axis=1, keepdims=True)


class Stream:
    def __init__(self, sources, slots, sems, block, steps):
        self.sources, self.slots, self.sems, self.block = sources, slots, sems, block
        self.steps, self.whole = steps, sources[0].shape[1] == block

    def copy(self, i, step):
        source = self.sources[i]
        if not self.whole:
            source = source.at[:, pl.ds(pl.multiple_of(step * self.block, self.block), self.block)]
        slot = lax.rem(step, 2)
        return pltpu.make_async_copy(source, self.slots[i].at[slot], self.sems.at[i, slot])

    def first(self):
        for i in range(len(self.sources)):
            self.copy(i, 0).start()

    def ahead(self, step):
        @pl.when(step + 1 < self.steps)
        def _():
            for i in range(len(self.sources)):
                self.copy(i, step + 1).start()

    def wait(self, i, step):
        self.copy(i, step).wait()
        return self.slots[i].at[lax.rem(step, 2)]


class Sink:
    def __init__(self, targets, slots, sems, block, steps, offset):
        self.targets, self.slots, self.sems, self.block = targets, slots, sems, block
        self.steps, self.offset, self.whole = steps, offset, targets[0].shape[1] == block

    def copy(self, i, step):
        target = self.targets[i]
        if not self.whole:
            target = target.at[:, pl.ds(pl.multiple_of((step + self.offset) * self.block, self.block), self.block)]
        slot = lax.rem(step, 2)
        return pltpu.make_async_copy(self.slots[i].at[slot], target, self.sems.at[i, slot])

    def put(self, i, step, value):
        @pl.when(step >= 2)
        def _():
            self.copy(i, step - 2).wait()

        self.slots[i].at[lax.rem(step, 2)][...] = value
        self.copy(i, step).start()

    def finish(self, step):
        @pl.when(step == self.steps - 1)
        def _():
            for i in range(len(self.targets)):
                if self.steps > 1:
                    self.copy(i, step - 1).wait()
                self.copy(i, step).wait()


def grad_slots(quarter, block):
    return [pltpu.VMEM((2, quarter, block), BF)] * 3 + [pltpu.SemaphoreType.DMA((3, 2))]


def derivatives(x_ref, u_ref, p, stream, step):
    x = x_ref[...]
    wg = stream.wait(0, step)
    pre_gate = dot(x, wg[...])
    wu = stream.wait(1, step)
    pre_up = dot(x, wu[...])
    wd = stream.wait(2, step)
    back = dot(u_ref[...], wd[...])
    s = jax.nn.sigmoid(pre_gate)
    activated = pre_gate * s
    hidden = (activated * pre_up).astype(BF)
    scaled_back = p * back
    d_gate = (scaled_back * pre_up * s * (1.0 + pre_gate * (1.0 - s))).astype(BF)
    d_up = (scaled_back * activated).astype(BF)
    return d_gate, d_up, hidden, back, wg, wu


def pieces_of(total, size):
    return [(a, min(size, total - a)) for a in range(0, total, size)]


def own_body(packed, early, groups, cap_ref, routes_ref, tok_hbm, out_hbm, wg_hbm, wu_hbm, wd_hbm, *refs):
    acts_refs, refs = (refs[:3], refs[3:]) if early is None else (refs[:4], refs[4:])
    (part_hbm, prob_ref, xq_hbm, sq_hbm, filled_ref, part_ref, xq_ref, sq_ref, tok_ref, out_ref, x_ref, u_ref, p_ref,
     table_ref, acc_ref, wg_ref, wu_ref, wd_ref, sems, row_sems, out_sems) = refs
    step = pl.program_id(0)
    width, block = wg_ref.shape[1:]
    quarter = xq_ref.shape[1]
    stream = Stream((wg_hbm, wu_hbm, wd_hbm), (wg_ref, wu_ref, wd_ref), sems, block, wg_hbm.shape[1] // block)
    owner, _, group = my_place(part_ref.shape[0])
    half = part_ref.shape[0] // 2
    halves = [pltpu.make_async_copy(part_ref.at[k * half:(k + 1) * half], part_hbm.at[k * half:(k + 1) * half],
                                    out_sems.at[k]) for k in range(2)]
    shares_out = [pltpu.make_async_copy(xq_ref, xq_hbm, out_sems.at[2]),
                  pltpu.make_async_copy(sq_ref, sq_hbm, out_sems.at[3])]

    @pl.when(step == 0)
    def _():
        rows = [pltpu.make_async_copy(tok_hbm, tok_ref, row_sems.at[0]),
                pltpu.make_async_copy(out_hbm, out_ref, row_sems.at[1])]
        rows[0].start()
        stream.copy(0, 0).start()
        rows[1].start()
        stream.copy(1, 0).start()
        stream.copy(2, 0).start()
        table, p = slot_table(routes_ref[...].astype(F32), owner, cap_ref[owner], (group == 1) & (groups == 2))
        table_ref[...] = table.astype(BF)
        p_ref[...] = p
        filled_ref[...] = jnp.sum(table, axis=1, keepdims=True)
        acc_ref[...] = jnp.zeros_like(acc_ref)
        prob_ref[...] = jnp.zeros_like(prob_ref)
        rows[0].wait()
        x_ref[...] = dot(table_ref[...], tok_ref[...]).astype(BF)
        rows[1].wait()
        u_ref[...] = dot(table_ref[...], out_ref[...]).astype(BF)
        at = pl.ds(pl.multiple_of(group * quarter, quarter), quarter)
        xq_ref[...] = x_ref[:, at]
        sq_ref[...] = (p * u_ref[:, at].astype(F32)).astype(BF)
        for copy in shares_out:
            copy.start()

    stream.ahead(step)
    d_gate, d_up, hidden, back, wg, wu = derivatives(x_ref, u_ref, p_ref[...], stream, step)
    acts = (d_gate, d_up, hidden)

    def store_early():
        for ref, value in zip(acts_refs, acts):
            ref[...] = value

    if early is None:
        store_early()
    else:
        pl.when(step < early)(store_early)

        @pl.when(step >= early)
        def _():
            for i, value in enumerate(acts):
                acts_refs[3][i] = value

    prob_ref[...] += jnp.sum(hidden.astype(F32) * back, axis=1, keepdims=True)
    gate_t = d_gate.T
    up_t = d_up.T
    for a, n in pieces_of(width, 512):
        at = slice(a, a + n)
        acc_ref[at, :] += dot(wg[at, :], gate_t) + dot(wu[at, :], up_t)

    @pl.when(step == pl.num_programs(0) - 1)
    def _():
        table = table_ref[...]
        count = table.shape[1]
        shares, _, fw = part_ref.shape
        by_slot = (((0,), (1,)), ((), ()))
        if packed:
            total = prob_ref[...]
            high = total.astype(BF).astype(F32)
            lane = lax.broadcasted_iota(jnp.int32, (CAP, 128), 1)
            both = jnp.where(lane == 0, high, jnp.where(lane == 1, total - high, 0.0)).astype(BF)
            by_token = dotg(both, table, FIRST)[:EXTRA].astype(BF)
        for j in range(shares):
            part_ref[j, :count, :] = dotg(table, acc_ref[j * fw:(j + 1) * fw, :].astype(BF), by_slot).astype(BF)
            if packed:
                part_ref[j, count:, :] = jnp.zeros((EXTRA, fw), BF)
                part_ref[j, count:, :count] = by_token
            if (j + 1) % half == 0:
                halves[j // half].start()
        for copy in halves + shares_out:
            copy.wait()


def weight_slots(width, block):
    return [pltpu.VMEM((2, width, block), BF)] * 3 + [pltpu.SemaphoreType.DMA((3, 2))]


def own_group(capacity, routes, tokens, grad_out, wg, wu, wd, shares, groups, packed, block, early):
    count, width = tokens.shape
    hidden = wg.shape[1]
    steps = hidden // block
    tall = count + (EXTRA if packed else 0)
    fw = width // shares
    quarter = width // groups
    act_specs = [pl.BlockSpec((CAP, block), lambda j: (0, jnp.minimum(j, early - 1)))] * 3
    acts = [jax.ShapeDtypeStruct((CAP, early * block), BF)] * 3
    if early < steps:
        act_specs.append(pl.BlockSpec((3, CAP, block), lambda j: (0, 0, jnp.maximum(j - early, 0))))
        acts.append(jax.ShapeDtypeStruct((3, CAP, (steps - early) * block), BF))
    column = jax.ShapeDtypeStruct((CAP, 1), F32)
    share = jax.ShapeDtypeStruct((CAP, quarter), BF)
    part = jax.ShapeDtypeStruct((shares, tall, fw), BF)
    rows = pltpu.VMEM((CAP, width), BF)
    tall_rows = pltpu.VMEM((count, width), BF)
    return pl.pallas_call(
        functools.partial(own_body, packed, early if early < steps else None, groups),
        grid=(steps,),
        in_specs=[whole_smem(), whole(routes.shape)] + [in_place()] * 5,
        out_specs=act_specs + [in_place(), whole(column.shape), in_place(), in_place(), whole(column.shape)],
        out_shape=acts + [part, column, share, share, column],
        scratch_shapes=[pltpu.VMEM(part.shape, BF)] + [pltpu.VMEM(share.shape, BF)] * 2 + [tall_rows, tall_rows, rows, rows, pltpu.VMEM((CAP, 1), F32), pltpu.VMEM((CAP, count), BF),
                        pltpu.VMEM((width, CAP), F32)] + weight_slots(width, block)
        + [pltpu.SemaphoreType.DMA((2,)), pltpu.SemaphoreType.DMA((4,))],
        compiler_params=params(),
        cost_estimate=pl.CostEstimate(
            flops=10 * CAP * width * hidden, bytes_accessed=6 * width * hidden, transcendentals=CAP * hidden),
        name="own_group",
    )(capacity, routes, tokens, grad_out, wg, wu, wd)


def joined(mine, other):
    return jnp.concatenate([mine, other], axis=0)


def merged(group, mine, other):
    first, last = jnp.where(group == 0, mine, other), jnp.where(group == 0, other, mine)
    lead = SHORT - CAP
    shared = CAP - lead
    return jnp.concatenate([first[:lead], first[lead:] + last[:shared], last[shared:]], axis=0)


def store_grads(groups, group, fits_ref, xs_ref, ss_ref, mine, other, sink, step):
    def grads(join, rows):
        for i, rows_ref in enumerate((xs_ref, xs_ref, ss_ref)):
            sink.put(i, step, dotg(rows_ref[:rows, :], join(mine(i), other(i)), FIRST).astype(BF))

    if groups == 2:
        @pl.when(fits_ref[0] == 1)
        def _():
            grads(functools.partial(merged, group), SHORT)

    @pl.when(fits_ref[0] == 0)
    def _():
        grads(joined, xs_ref.shape[0])

    sink.finish(step)


def again_body(groups, shares, steps, cap_ref, xq_ref, sq_ref, filled_ref, one_hbm, two_hbm, dg_ref, du_ref, h_ref,
               wg_hbm, wu_hbm, wd_hbm, gg_hbm, gu_hbm, gd_hbm, xs_hbm, ss_hbm, fits_ref,
               xs_ref, ss_ref, one_ref, two_ref, xo_ref, uo_ref, po_ref, wg_ref, wu_ref, wd_ref, sems,
               gg_ref, gu_ref, gd_ref, out_sems, row_sems):
    step = pl.program_id(0)
    owner, parity, group = my_place(shares)
    quarter = xs_ref.shape[1]
    count = one_ref.shape[1] - EXTRA
    stream = Stream((wg_hbm, wu_hbm, wd_hbm), (wg_ref, wu_ref, wd_ref), sems, wg_ref.shape[2], steps)
    sink = Sink((gg_hbm, gu_hbm, gd_hbm), (gg_ref, gu_ref, gd_ref), out_sems, wg_ref.shape[2], steps, 0)
    joint = [pltpu.make_async_copy(xs_ref, xs_hbm, row_sems.at[2]), pltpu.make_async_copy(ss_ref, ss_hbm, row_sems.at[3])]

    @pl.when(step == 0)
    def _():
        rows = [pltpu.make_async_copy(one_hbm, one_ref, row_sems.at[0]),
                pltpu.make_async_copy(two_hbm, two_ref, row_sems.at[1])]
        for copy in rows:
            copy.start()
        stream.first()
        for copy in rows:
            copy.wait()
        filled = jnp.sum(filled_ref[...])
        for g in range(groups - 1):
            at = slice(g * CAP, (g + 1) * CAP)
            routes = one_ref[g, count:count + EXTRA, :count].astype(F32)
            table, p = slot_table(routes, owner, cap_ref[owner], (group == 0) & (groups == 2))
            filled += jnp.sum(table)
            po_ref[at, :] = p
            table = table.astype(BF)
            from_one = dot(table, one_ref[g, :count, :]).astype(BF)
            from_two = dot(table, two_ref[g, :count, :]).astype(BF)

            @pl.when(parity == 0)
            def _():
                xo_ref[at, :] = from_one
                uo_ref[at, :] = from_two

            @pl.when(parity == 1)
            def _():
                xo_ref[at, :] = from_two
                uo_ref[at, :] = from_one

        fits = filled <= SHORT if groups == 2 else jnp.bool_(False)
        fits_ref[0] = fits.astype(jnp.int32)
        part = pl.ds(pl.multiple_of(group * quarter, quarter), quarter)
        mine, scaled = xq_ref[...], sq_ref[...]
        other = xo_ref[:, part]
        scaled_other = (po_ref[...] * uo_ref[:, part].astype(F32)).astype(BF)
        if groups == 2:
            @pl.when(fits)
            def _():
                xs_ref[:SHORT, :] = merged(group, mine, other)
                ss_ref[:SHORT, :] = merged(group, scaled, scaled_other)

        @pl.when(jnp.logical_not(fits))
        def _():
            xs_ref[...] = joined(mine, other)
            ss_ref[...] = joined(scaled, scaled_other)

        for copy in joint:
            copy.start()

    stream.ahead(step)
    acts = derivatives(xo_ref, uo_ref, po_ref[...], stream, step)
    own = (dg_ref, du_ref, h_ref)
    store_grads(groups, group, fits_ref, xs_ref, ss_ref, lambda i: own[i][...], lambda i: acts[i], sink, step)

    @pl.when(step == steps - 1)
    def _():
        for copy in joint:
            copy.wait()


def grads_again(capacity, xq, sq, filled, one, two, dg, du, h, wg, wu, wd, groups, shares, block):
    width, hidden = wg.shape
    others = (groups - 1) * CAP
    quarter = width // groups
    steps = dg.shape[1] // block
    act = pl.BlockSpec((CAP, block), lambda j: (0, j))
    arrived = pltpu.VMEM(one.shape, BF)
    rows = pltpu.VMEM((others, width), BF)
    joint = jax.ShapeDtypeStruct((CAP + others, quarter), BF)
    return pl.pallas_call(
        functools.partial(again_body, groups, shares, steps),
        grid=(steps,),
        in_specs=[whole_smem(), whole(xq.shape), whole(sq.shape), whole(filled.shape), in_place(), in_place(),
                  act, act, act, in_place(), in_place(), in_place()],
        out_specs=[in_place()] * 5 + [whole_smem()],
        out_shape=[jax.ShapeDtypeStruct((quarter, hidden), BF)] * 3 + [joint] * 2 + [jax.ShapeDtypeStruct((1,), jnp.int32)],
        scratch_shapes=[pltpu.VMEM(joint.shape, BF)] * 2 + [arrived, arrived, rows, rows, pltpu.VMEM((others, 1), F32)]
        + weight_slots(width, block) + grad_slots(quarter, block) + [pltpu.SemaphoreType.DMA((4,))],
        compiler_params=params(),
        cost_estimate=pl.CostEstimate(
            flops=(6 * others * width + 6 * (CAP + others) * quarter) * steps * block,
            bytes_accessed=6 * (width + quarter) * steps * block, transcendentals=others * steps * block),
        name="grads_again",
    )(capacity, xq, sq, filled, one, two, dg, du, h, wg, wu, wd)


def given_body(groups, shares, steps, fits_ref, xs_ref, ss_ref, mine_ref, other_ref, gg_in, gu_in, gd_in, gg_hbm, gu_hbm, gd_hbm,
               gg_ref, gu_ref, gd_ref, out_sems):
    _, _, group = my_place(shares)
    step = pl.program_id(0)
    block = gg_ref.shape[2]
    sink = Sink((gg_hbm, gu_hbm, gd_hbm), (gg_ref, gu_ref, gd_ref), out_sems, block, steps, gg_hbm.shape[1] // block - steps)
    store_grads(groups, group, fits_ref, xs_ref, ss_ref, lambda i: mine_ref[i], lambda i: other_ref[i], sink, step)


def grads_given(fits, xs, ss, mine, other, grads, groups, shares, block):
    quarter, hidden = grads[0].shape
    steps = mine.shape[2] // block
    act = pl.BlockSpec((3, CAP, block), lambda j: (0, 0, j))
    return pl.pallas_call(
        functools.partial(given_body, groups, shares, steps),
        grid=(steps,),
        in_specs=[whole_smem(), whole(xs.shape), whole(ss.shape), act, act] + [in_place()] * 3,
        out_specs=[in_place()] * 3,
        out_shape=[jax.ShapeDtypeStruct((quarter, hidden), BF)] * 3,
        scratch_shapes=grad_slots(quarter, block),
        input_output_aliases={5: 0, 6: 1, 7: 2},
        compiler_params=params(),
        cost_estimate=pl.CostEstimate(
            flops=6 * xs.shape[0] * quarter * steps * block, bytes_accessed=6 * quarter * steps * block, transcendentals=0),
        name="grads_given",
    )(fits, xs, ss, mine, other, *grads)


def block_of(hidden, largest):
    for size in (512, 256, 128):
        if size <= largest and hidden % size == 0:
            return size
    return hidden


def per_device(tokens, grad_out, gate_probs, expert_ids, capacity, w_gate, w_up, w_down):
    groups = lax.axis_size("expert")
    shares = lax.axis_size("dp")
    count, width = tokens.shape
    hidden = w_gate.shape[1]
    per_expert = shares // EXPERTS
    packed = width // shares >= count
    block = block_of(hidden, 512)
    steps = hidden // block
    early = steps - steps * 3 // 7 if groups == 2 else steps

    routes, send = pack(expert_ids.T, gate_probs.T, tokens, grad_out, shares)
    arounds = [[(i, (i + shift) % groups) for i in range(groups)] for shift in range(1, groups)]
    one = [lax.ppermute(send, "expert", around) for around in arounds]

    *acts, part, prob, xq, sq, filled = own_group(
        capacity, routes, tokens, grad_out, w_gate, w_up, w_down, shares, groups, packed, block, early)

    one, part = lax.optimization_barrier((one, part))
    swap = [(i, i ^ 1) for i in range(shares)]
    two = [lax.ppermute(rows, "dp", swap) for rows in one]
    if early < steps:
        late = acts.pop()
        late_other = lax.ppermute(late, "expert", arounds[0])
    arrived = lax.all_to_all(part, "dp", split_axis=0, concat_axis=0, tiled=True)

    def stacked(parts):
        return parts[0][None] if len(parts) == 1 else jnp.stack(parts)

    *grads, xs, ss, fits = grads_again(
        capacity, xq, sq, filled, stacked(one), stacked(two), *acts, w_gate, w_up, w_down, groups, shares, block)
    if early < steps:
        grads = grads_given(fits, xs, ss, late, late_other, grads, groups, shares, block)
    grad_gate, grad_up, grad_down = grads

    token_grad = jnp.sum(arrived[:, :count].astype(F32), axis=0).astype(BF)
    if packed:
        ends = arrived[:, count:count + 2, :count].astype(F32)
        by_expert = jnp.sum(ends.reshape(EXPERTS, per_expert * 2, count), axis=1)
    else:
        owner, _, group = my_place(shares)
        table, _ = slot_table(routes.astype(F32), owner, capacity[owner], (group == 1) & (groups == 2))
        mine = jnp.sum(table * prob, axis=0)
        one_hot = (jnp.arange(EXPERTS) == owner).astype(F32)
        by_expert = lax.psum(one_hot[:, None] * mine[None, :], "dp")
    match = expert_ids[:, :, None] == jnp.arange(EXPERTS, dtype=jnp.int32)
    prob_grad = jnp.sum(jnp.where(match, by_expert.T[:, None, :], 0.0), axis=2).astype(BF)
    return (token_grad, prob_grad, grad_gate, grad_up, grad_down)


def solution(mesh):
    return jax.shard_map(
        per_device,
        mesh=mesh,
        in_specs=(
            P("expert", None),
            P("expert", None),
            P("expert", None),
            P("expert", None),
            P(),
            P(None, "dp"),
            P(None, "dp"),
            P(None, "dp"),
        ),
        out_specs=(
            P("expert", "dp"),
            P("expert", None),
            P("expert", "dp"),
            P("expert", "dp"),
            P("expert", "dp"),
        ),
        check_vma=False,
    )
```

```python
import functools

import jax
import jax.numpy as jnp
from jax import lax
from jax.experimental import pallas as pl
from jax.experimental.pallas import tpu as pltpu
from jax.sharding import PartitionSpec as P

EXPERTS = 4
CAP = 144
SHORT = 256
EXTRA = 16
BF = jnp.bfloat16
F32 = jnp.float32
VMEM_LIMIT = 60 * 1024 * 1024

FIRST = (((0,), (0,)), ((), ()))
LAST = (((1,), (1,)), ((), ()))


def dot(a, b):
    return jnp.dot(a, b, preferred_element_type=F32)


def dotg(a, b, dims):
    return lax.dot_general(a, b, dims, preferred_element_type=F32)


def whole(shape):
    return pl.BlockSpec(shape, lambda *_: (0,) * len(shape), pipeline_mode=pl.Buffered(1))


def params():
    return pltpu.CompilerParams(vmem_limit_bytes=VMEM_LIMIT)


def whole_smem():
    return pl.BlockSpec(memory_space=pltpu.SMEM)


def in_place():
    return pl.BlockSpec(memory_space=pl.ANY)


def my_place(shares):
    index = lax.axis_index("dp")
    return index // (shares // EXPERTS), index % 2, lax.axis_index("expert")


def pack_body(shares, ids_ref, probs_ref, tok_hbm, out_hbm, routes_ref, send_ref, sem):
    _, parity, _ = my_place(shares)
    count = tok_hbm.shape[0]
    top = send_ref.at[:count]

    @pl.when(parity == 0)
    def _():
        pltpu.make_async_copy(tok_hbm, top, sem).start()

    @pl.when(parity == 1)
    def _():
        pltpu.make_async_copy(out_hbm, top, sem).start()

    ids = ids_ref[...].astype(F32)
    routes = jnp.concatenate([ids, probs_ref[...].astype(F32), jnp.zeros((EXTRA - 4, count), F32)], axis=0).astype(BF)
    routes_ref[...] = routes
    send_ref[count:, :] = jnp.zeros((EXTRA, send_ref.shape[1]), BF)
    send_ref[count:, :count] = routes
    pltpu.make_async_copy(tok_hbm, top, sem).wait()


def pack(ids, probs, tokens, grad_out, shares):
    count, width = tokens.shape
    return pl.pallas_call(
        functools.partial(pack_body, shares),
        in_specs=[whole(ids.shape), whole(probs.shape), in_place(), in_place()],
        out_specs=[whole((EXTRA, count)), whole((count + EXTRA, width))],
        out_shape=[jax.ShapeDtypeStruct((EXTRA, count), BF), jax.ShapeDtypeStruct((count + EXTRA, width), BF)],
        scratch_shapes=[pltpu.SemaphoreType.DMA(())],
        compiler_params=params(),
        cost_estimate=pl.CostEstimate(flops=0, bytes_accessed=4 * count * width, transcendentals=0),
        name="pack",
    )(ids, probs, tokens, grad_out)


def slot_table(routes, owner, limit, backwards):
    count = routes.shape[1]
    hit = (routes[:2] == owner.astype(F32)).astype(F32)
    named = jnp.sum(hit, axis=0, keepdims=True)
    weight = jnp.sum(hit * routes[2:4], axis=0, keepdims=True)
    row = lax.broadcasted_iota(jnp.int32, (count, count), 0)
    col = lax.broadcasted_iota(jnp.int32, (count, count), 1)
    earlier = (row < col).astype(F32).astype(BF)
    wide = jnp.broadcast_to(named, (16, count)).astype(BF)
    rank = dot(wide, earlier)[:1].astype(jnp.int32)
    kept = (named > 0) & (rank < limit)
    slot = lax.broadcasted_iota(jnp.int32, (CAP, count), 0)
    slot = jnp.where(backwards, CAP - 1 - slot, slot)
    table = ((slot == rank) & kept).astype(F32)
    return table, jnp.sum(table * weight, axis=1, keepdims=True)


class Stream:
    def __init__(self, sources, slots, sems, block, steps):
        self.sources, self.slots, self.sems, self.block = sources, slots, sems, block
        self.steps, self.whole = steps, sources[0].shape[1] == block

    def copy(self, i, step):
        source = self.sources[i]
        if not self.whole:
            source = source.at[:, pl.ds(pl.multiple_of(step * self.block, self.block), self.block)]
        slot = lax.rem(step, 2)
        return pltpu.make_async_copy(source, self.slots[i].at[slot], self.sems.at[i, slot])

    def first(self):
        for i in range(len(self.sources)):
            self.copy(i, 0).start()

    def ahead(self, step):
        @pl.when(step + 1 < self.steps)
        def _():
            for i in range(len(self.sources)):
                self.copy(i, step + 1).start()

    def wait(self, i, step):
        self.copy(i, step).wait()
        return self.slots[i].at[lax.rem(step, 2)]


def derivatives(x_ref, u_ref, p, stream, step):
    x = x_ref[...]
    wg = stream.wait(0, step)
    pre_gate = dot(x, wg[...])
    wu = stream.wait(1, step)
    pre_up = dot(x, wu[...])
    wd = stream.wait(2, step)
    back = dot(u_ref[...], wd[...])
    s = jax.nn.sigmoid(pre_gate)
    activated = pre_gate * s
    hidden = (activated * pre_up).astype(BF)
    scaled_back = p * back
    d_gate = (scaled_back * pre_up * s * (1.0 + pre_gate * (1.0 - s))).astype(BF)
    d_up = (scaled_back * activated).astype(BF)
    return d_gate, d_up, hidden, back, wg, wu


def pieces_of(total, size):
    return [(a, min(size, total - a)) for a in range(0, total, size)]


def own_body(packed, early, groups, cap_ref, routes_ref, tok_hbm, out_hbm, wg_hbm, wu_hbm, wd_hbm, *refs):
    acts_refs, refs = (refs[:3], refs[3:]) if early is None else (refs[:4], refs[4:])
    (part_hbm, prob_ref, xq_hbm, sq_hbm, filled_ref, part_ref, xq_ref, sq_ref, tok_ref, out_ref, x_ref, u_ref, p_ref,
     table_ref, acc_ref, wg_ref, wu_ref, wd_ref, sems, row_sems, out_sems) = refs
    step = pl.program_id(0)
    width, block = wg_ref.shape[1:]
    quarter = xq_ref.shape[1]
    stream = Stream((wg_hbm, wu_hbm, wd_hbm), (wg_ref, wu_ref, wd_ref), sems, block, wg_hbm.shape[1] // block)
    owner, _, group = my_place(part_ref.shape[0])
    half = part_ref.shape[0] // 2
    halves = [pltpu.make_async_copy(part_ref.at[k * half:(k + 1) * half], part_hbm.at[k * half:(k + 1) * half],
                                    out_sems.at[k]) for k in range(2)]
    shares_out = [pltpu.make_async_copy(xq_ref, xq_hbm, out_sems.at[2]),
                  pltpu.make_async_copy(sq_ref, sq_hbm, out_sems.at[3])]

    @pl.when(step == 0)
    def _():
        rows = [pltpu.make_async_copy(tok_hbm, tok_ref, row_sems.at[0]),
                pltpu.make_async_copy(out_hbm, out_ref, row_sems.at[1])]
        rows[0].start()
        stream.copy(0, 0).start()
        rows[1].start()
        stream.copy(1, 0).start()
        stream.copy(2, 0).start()
        table, p = slot_table(routes_ref[...].astype(F32), owner, cap_ref[owner], (group == 1) & (groups == 2))
        table_ref[...] = table.astype(BF)
        p_ref[...] = p
        filled_ref[...] = jnp.sum(table, axis=1, keepdims=True)
        acc_ref[...] = jnp.zeros_like(acc_ref)
        prob_ref[...] = jnp.zeros_like(prob_ref)
        rows[0].wait()
        x_ref[...] = dot(table_ref[...], tok_ref[...]).astype(BF)
        rows[1].wait()
        u_ref[...] = dot(table_ref[...], out_ref[...]).astype(BF)
        at = pl.ds(pl.multiple_of(group * quarter, quarter), quarter)
        xq_ref[...] = x_ref[:, at]
        sq_ref[...] = (p * u_ref[:, at].astype(F32)).astype(BF)
        for copy in shares_out:
            copy.start()

    stream.ahead(step)
    d_gate, d_up, hidden, back, wg, wu = derivatives(x_ref, u_ref, p_ref[...], stream, step)
    acts = (d_gate, d_up, hidden)

    def store_early():
        for ref, value in zip(acts_refs, acts):
            ref[...] = value

    if early is None:
        store_early()
    else:
        pl.when(step < early)(store_early)

        @pl.when(step >= early)
        def _():
            for i, value in enumerate(acts):
                acts_refs[3][i] = value

    prob_ref[...] += jnp.sum(hidden.astype(F32) * back, axis=1, keepdims=True)
    gate_t = d_gate.T
    up_t = d_up.T
    for a, n in pieces_of(width, 512):
        at = slice(a, a + n)
        acc_ref[at, :] += dot(wg[at, :], gate_t) + dot(wu[at, :], up_t)

    @pl.when(step == pl.num_programs(0) - 1)
    def _():
        table = table_ref[...]
        count = table.shape[1]
        shares, _, fw = part_ref.shape
        by_slot = (((0,), (1,)), ((), ()))
        if packed:
            total = prob_ref[...]
            high = total.astype(BF).astype(F32)
            lane = lax.broadcasted_iota(jnp.int32, (CAP, 128), 1)
            both = jnp.where(lane == 0, high, jnp.where(lane == 1, total - high, 0.0)).astype(BF)
            by_token = dotg(both, table, FIRST)[:EXTRA].astype(BF)
        for j in range(shares):
            part_ref[j, :count, :] = dotg(table, acc_ref[j * fw:(j + 1) * fw, :].astype(BF), by_slot).astype(BF)
            if packed:
                part_ref[j, count:, :] = jnp.zeros((EXTRA, fw), BF)
                part_ref[j, count:, :count] = by_token
            if (j + 1) % half == 0:
                halves[j // half].start()
        for copy in halves + shares_out:
            copy.wait()


def weight_slots(width, block):
    return [pltpu.VMEM((2, width, block), BF)] * 3 + [pltpu.SemaphoreType.DMA((3, 2))]


def own_group(capacity, routes, tokens, grad_out, wg, wu, wd, shares, groups, packed, block, early):
    count, width = tokens.shape
    hidden = wg.shape[1]
    steps = hidden // block
    tall = count + (EXTRA if packed else 0)
    fw = width // shares
    quarter = width // groups
    act_specs = [pl.BlockSpec((CAP, block), lambda j: (0, jnp.minimum(j, early - 1)))] * 3
    acts = [jax.ShapeDtypeStruct((CAP, early * block), BF)] * 3
    if early < steps:
        act_specs.append(pl.BlockSpec((3, CAP, block), lambda j: (0, 0, jnp.maximum(j - early, 0))))
        acts.append(jax.ShapeDtypeStruct((3, CAP, (steps - early) * block), BF))
    column = jax.ShapeDtypeStruct((CAP, 1), F32)
    share = jax.ShapeDtypeStruct((CAP, quarter), BF)
    part = jax.ShapeDtypeStruct((shares, tall, fw), BF)
    rows = pltpu.VMEM((CAP, width), BF)
    tall_rows = pltpu.VMEM((count, width), BF)
    return pl.pallas_call(
        functools.partial(own_body, packed, early if early < steps else None, groups),
        grid=(steps,),
        in_specs=[whole_smem(), whole(routes.shape)] + [in_place()] * 5,
        out_specs=act_specs + [in_place(), whole(column.shape), in_place(), in_place(), whole(column.shape)],
        out_shape=acts + [part, column, share, share, column],
        scratch_shapes=[pltpu.VMEM(part.shape, BF)] + [pltpu.VMEM(share.shape, BF)] * 2 + [tall_rows, tall_rows, rows, rows, pltpu.VMEM((CAP, 1), F32), pltpu.VMEM((CAP, count), BF),
                        pltpu.VMEM((width, CAP), F32)] + weight_slots(width, block)
        + [pltpu.SemaphoreType.DMA((2,)), pltpu.SemaphoreType.DMA((4,))],
        compiler_params=params(),
        cost_estimate=pl.CostEstimate(
            flops=10 * CAP * width * hidden, bytes_accessed=6 * width * hidden, transcendentals=CAP * hidden),
        name="own_group",
    )(capacity, routes, tokens, grad_out, wg, wu, wd)


def joined(mine, other):
    return jnp.concatenate([mine, other], axis=0)


def merged(group, mine, other):
    first, last = jnp.where(group == 0, mine, other), jnp.where(group == 0, other, mine)
    lead = SHORT - CAP
    shared = CAP - lead
    return jnp.concatenate([first[:lead], first[lead:] + last[:shared], last[shared:]], axis=0)


def store_grads(groups, group, fits_ref, xs_ref, ss_ref, mine, other, out_refs):
    def grads(join, rows):
        for i, (rows_ref, out_ref) in enumerate(zip((xs_ref, xs_ref, ss_ref), out_refs)):
            out_ref[...] = dotg(rows_ref[:rows, :], join(mine(i), other(i)), FIRST).astype(BF)

    if groups == 2:
        @pl.when(fits_ref[0] == 1)
        def _():
            grads(functools.partial(merged, group), SHORT)

    @pl.when(fits_ref[0] == 0)
    def _():
        grads(joined, xs_ref.shape[0])


def again_body(groups, shares, steps, cap_ref, xq_ref, sq_ref, filled_ref, one_hbm, two_hbm, dg_ref, du_ref, h_ref,
               wg_hbm, wu_hbm, wd_hbm, gg_ref, gu_ref, gd_ref, xs_hbm, ss_hbm, fits_ref,
               xs_ref, ss_ref, one_ref, two_ref, xo_ref, uo_ref, po_ref, wg_ref, wu_ref, wd_ref, sems, row_sems):
    step = pl.program_id(0)
    owner, parity, group = my_place(shares)
    quarter = xs_ref.shape[1]
    count = one_ref.shape[1] - EXTRA
    stream = Stream((wg_hbm, wu_hbm, wd_hbm), (wg_ref, wu_ref, wd_ref), sems, wg_ref.shape[2], steps)
    joint = [pltpu.make_async_copy(xs_ref, xs_hbm, row_sems.at[2]), pltpu.make_async_copy(ss_ref, ss_hbm, row_sems.at[3])]

    @pl.when(step == 0)
    def _():
        rows = [pltpu.make_async_copy(one_hbm, one_ref, row_sems.at[0]),
                pltpu.make_async_copy(two_hbm, two_ref, row_sems.at[1])]
        for copy in rows:
            copy.start()
        stream.first()
        for copy in rows:
            copy.wait()
        filled = jnp.sum(filled_ref[...])
        for g in range(groups - 1):
            at = slice(g * CAP, (g + 1) * CAP)
            routes = one_ref[g, count:count + EXTRA, :count].astype(F32)
            table, p = slot_table(routes, owner, cap_ref[owner], (group == 0) & (groups == 2))
            filled += jnp.sum(table)
            po_ref[at, :] = p
            table = table.astype(BF)
            from_one = dot(table, one_ref[g, :count, :]).astype(BF)
            from_two = dot(table, two_ref[g, :count, :]).astype(BF)

            @pl.when(parity == 0)
            def _():
                xo_ref[at, :] = from_one
                uo_ref[at, :] = from_two

            @pl.when(parity == 1)
            def _():
                xo_ref[at, :] = from_two
                uo_ref[at, :] = from_one

        fits = filled <= SHORT if groups == 2 else jnp.bool_(False)
        fits_ref[0] = fits.astype(jnp.int32)
        part = pl.ds(pl.multiple_of(group * quarter, quarter), quarter)
        mine, scaled = xq_ref[...], sq_ref[...]
        other = xo_ref[:, part]
        scaled_other = (po_ref[...] * uo_ref[:, part].astype(F32)).astype(BF)
        if groups == 2:
            @pl.when(fits)
            def _():
                xs_ref[:SHORT, :] = merged(group, mine, other)
                ss_ref[:SHORT, :] = merged(group, scaled, scaled_other)

        @pl.when(jnp.logical_not(fits))
        def _():
            xs_ref[...] = joined(mine, other)
            ss_ref[...] = joined(scaled, scaled_other)

        for copy in joint:
            copy.start()

    stream.ahead(step)
    acts = derivatives(xo_ref, uo_ref, po_ref[...], stream, step)
    own = (dg_ref, du_ref, h_ref)
    store_grads(groups, group, fits_ref, xs_ref, ss_ref, lambda i: own[i][...], lambda i: acts[i], (gg_ref, gu_ref, gd_ref))

    @pl.when(step == steps - 1)
    def _():
        for copy in joint:
            copy.wait()


def grads_again(capacity, xq, sq, filled, one, two, dg, du, h, wg, wu, wd, groups, shares, block):
    width, hidden = wg.shape
    others = (groups - 1) * CAP
    quarter = width // groups
    steps = dg.shape[1] // block
    act = pl.BlockSpec((CAP, block), lambda j: (0, j))
    grad = pl.BlockSpec((quarter, block), lambda j: (0, j))
    arrived = pltpu.VMEM(one.shape, BF)
    rows = pltpu.VMEM((others, width), BF)
    joint = jax.ShapeDtypeStruct((CAP + others, quarter), BF)
    return pl.pallas_call(
        functools.partial(again_body, groups, shares, steps),
        grid=(steps,),
        in_specs=[whole_smem(), whole(xq.shape), whole(sq.shape), whole(filled.shape), in_place(), in_place(),
                  act, act, act, in_place(), in_place(), in_place()],
        out_specs=[grad] * 3 + [in_place()] * 2 + [whole_smem()],
        out_shape=[jax.ShapeDtypeStruct((quarter, hidden), BF)] * 3 + [joint] * 2 + [jax.ShapeDtypeStruct((1,), jnp.int32)],
        scratch_shapes=[pltpu.VMEM(joint.shape, BF)] * 2 + [arrived, arrived, rows, rows, pltpu.VMEM((others, 1), F32)]
        + weight_slots(width, block) + [pltpu.SemaphoreType.DMA((4,))],
        compiler_params=params(),
        cost_estimate=pl.CostEstimate(
            flops=(6 * others * width + 6 * (CAP + others) * quarter) * steps * block,
            bytes_accessed=6 * (width + quarter) * steps * block, transcendentals=others * steps * block),
        name="grads_again",
    )(capacity, xq, sq, filled, one, two, dg, du, h, wg, wu, wd)


def given_body(groups, shares, fits_ref, xs_ref, ss_ref, mine_ref, other_ref, gg_in, gu_in, gd_in, gg_ref, gu_ref, gd_ref):
    _, _, group = my_place(shares)
    store_grads(groups, group, fits_ref, xs_ref, ss_ref, lambda i: mine_ref[i], lambda i: other_ref[i], (gg_ref, gu_ref, gd_ref))


def grads_given(fits, xs, ss, mine, other, grads, groups, shares, block):
    quarter, hidden = grads[0].shape
    steps = mine.shape[2] // block
    early = hidden // block - steps
    grad = pl.BlockSpec((quarter, block), lambda j: (0, j + early))
    act = pl.BlockSpec((3, CAP, block), lambda j: (0, 0, j))
    return pl.pallas_call(
        functools.partial(given_body, groups, shares),
        grid=(steps,),
        in_specs=[whole_smem(), whole(xs.shape), whole(ss.shape), act, act] + [in_place()] * 3,
        out_specs=[grad] * 3,
        out_shape=[jax.ShapeDtypeStruct((quarter, hidden), BF)] * 3,
        input_output_aliases={5: 0, 6: 1, 7: 2},
        compiler_params=params(),
        cost_estimate=pl.CostEstimate(
            flops=6 * xs.shape[0] * quarter * steps * block, bytes_accessed=6 * quarter * steps * block, transcendentals=0),
        name="grads_given",
    )(fits, xs, ss, mine, other, *grads)


def block_of(hidden, largest):
    for size in (512, 256, 128):
        if size <= largest and hidden % size == 0:
            return size
    return hidden


def per_device(tokens, grad_out, gate_probs, expert_ids, capacity, w_gate, w_up, w_down):
    groups = lax.axis_size("expert")
    shares = lax.axis_size("dp")
    count, width = tokens.shape
    hidden = w_gate.shape[1]
    per_expert = shares // EXPERTS
    packed = width // shares >= count
    block = block_of(hidden, 512)
    steps = hidden // block
    early = steps - steps * 3 // 7 if groups == 2 else steps

    routes, send = pack(expert_ids.T, gate_probs.T, tokens, grad_out, shares)
    arounds = [[(i, (i + shift) % groups) for i in range(groups)] for shift in range(1, groups)]
    one = [lax.ppermute(send, "expert", around) for around in arounds]

    *acts, part, prob, xq, sq, filled = own_group(
        capacity, routes, tokens, grad_out, w_gate, w_up, w_down, shares, groups, packed, block, early)

    one, part = lax.optimization_barrier((one, part))
    swap = [(i, i ^ 1) for i in range(shares)]
    two = [lax.ppermute(rows, "dp", swap) for rows in one]
    if early < steps:
        late = acts.pop()
        late_other = lax.ppermute(late, "expert", arounds[0])
    arrived = lax.all_to_all(part, "dp", split_axis=0, concat_axis=0, tiled=True)

    def stacked(parts):
        return parts[0][None] if len(parts) == 1 else jnp.stack(parts)

    *grads, xs, ss, fits = grads_again(
        capacity, xq, sq, filled, stacked(one), stacked(two), *acts, w_gate, w_up, w_down, groups, shares, block)
    if early < steps:
        grads = grads_given(fits, xs, ss, late, late_other, grads, groups, shares, block)
    grad_gate, grad_up, grad_down = grads

    token_grad = jnp.sum(arrived[:, :count].astype(F32), axis=0).astype(BF)
    if packed:
        ends = arrived[:, count:count + 2, :count].astype(F32)
        by_expert = jnp.sum(ends.reshape(EXPERTS, per_expert * 2, count), axis=1)
    else:
        owner, _, group = my_place(shares)
        table, _ = slot_table(routes.astype(F32), owner, capacity[owner], (group == 1) & (groups == 2))
        mine = jnp.sum(table * prob, axis=0)
        one_hot = (jnp.arange(EXPERTS) == owner).astype(F32)
        by_expert = lax.psum(one_hot[:, None] * mine[None, :], "dp")
    match = expert_ids[:, :, None] == jnp.arange(EXPERTS, dtype=jnp.int32)
    prob_grad = jnp.sum(jnp.where(match, by_expert.T[:, None, :], 0.0), axis=2).astype(BF)
    return (token_grad, prob_grad, grad_gate, grad_up, grad_down)


def solution(mesh):
    return jax.shard_map(
        per_device,
        mesh=mesh,
        in_specs=(
            P("expert", None),
            P("expert", None),
            P("expert", None),
            P("expert", None),
            P(),
            P(None, "dp"),
            P(None, "dp"),
            P(None, "dp"),
        ),
        out_specs=(
            P("expert", "dp"),
            P("expert", None),
            P("expert", "dp"),
            P("expert", "dp"),
            P("expert", "dp"),
        ),
        check_vma=False,
    )
```

```python
import functools

import jax
import jax.numpy as jnp
from jax import lax
from jax.experimental import pallas as pl
from jax.experimental.pallas import tpu as pltpu
from jax.sharding import PartitionSpec as P

EXPERTS = 4
CAP = 144
SHORT = 256
EXTRA = 16
BF = jnp.bfloat16
F32 = jnp.float32
MIB = 1024 * 1024
KEPT = 2

FIRST = (((0,), (0,)), ((), ()))
LAST = (((1,), (1,)), ((), ()))


def dot(a, b):
    return jnp.dot(a, b, preferred_element_type=F32)


def dotg(a, b, dims):
    return lax.dot_general(a, b, dims, preferred_element_type=F32)


def whole(shape):
    return pl.BlockSpec(shape, lambda *_: (0,) * len(shape), pipeline_mode=pl.Buffered(1))


def params(mib=60):
    return pltpu.CompilerParams(vmem_limit_bytes=mib * MIB)


def whole_smem():
    return pl.BlockSpec(memory_space=pltpu.SMEM)


def in_place():
    return pl.BlockSpec(memory_space=pl.ANY)


def my_place(shares):
    index = lax.axis_index("dp")
    return index // (shares // EXPERTS), index % 2, lax.axis_index("expert")


def pack_body(shares, ids_ref, probs_ref, tok_hbm, out_hbm, routes_ref, send_ref, sem):
    _, parity, _ = my_place(shares)
    count = tok_hbm.shape[0]
    top = send_ref.at[:count]

    @pl.when(parity == 0)
    def _():
        pltpu.make_async_copy(tok_hbm, top, sem).start()

    @pl.when(parity == 1)
    def _():
        pltpu.make_async_copy(out_hbm, top, sem).start()

    ids = ids_ref[...].astype(F32)
    routes = jnp.concatenate([ids, probs_ref[...].astype(F32), jnp.zeros((EXTRA - 4, count), F32)], axis=0).astype(BF)
    routes_ref[...] = routes
    send_ref[count:, :] = jnp.zeros((EXTRA, send_ref.shape[1]), BF)
    send_ref[count:, :count] = routes
    pltpu.make_async_copy(tok_hbm, top, sem).wait()


def pack(ids, probs, tokens, grad_out, shares):
    count, width = tokens.shape
    return pl.pallas_call(
        functools.partial(pack_body, shares),
        in_specs=[whole(ids.shape), whole(probs.shape), in_place(), in_place()],
        out_specs=[whole((EXTRA, count)), whole((count + EXTRA, width))],
        out_shape=[jax.ShapeDtypeStruct((EXTRA, count), BF), jax.ShapeDtypeStruct((count + EXTRA, width), BF)],
        scratch_shapes=[pltpu.SemaphoreType.DMA(())],
        compiler_params=params(),
        cost_estimate=pl.CostEstimate(flops=0, bytes_accessed=4 * count * width, transcendentals=0),
        name="pack",
    )(ids, probs, tokens, grad_out)


def slot_table(routes, owner, limit, backwards):
    count = routes.shape[1]
    hit = (routes[:2] == owner.astype(F32)).astype(F32)
    named = jnp.sum(hit, axis=0, keepdims=True)
    weight = jnp.sum(hit * routes[2:4], axis=0, keepdims=True)
    row = lax.broadcasted_iota(jnp.int32, (count, count), 0)
    col = lax.broadcasted_iota(jnp.int32, (count, count), 1)
    earlier = (row < col).astype(F32).astype(BF)
    wide = jnp.broadcast_to(named, (16, count)).astype(BF)
    rank = dot(wide, earlier)[:1].astype(jnp.int32)
    kept = (named > 0) & (rank < limit)
    slot = lax.broadcasted_iota(jnp.int32, (CAP, count), 0)
    slot = jnp.where(backwards, CAP - 1 - slot, slot)
    table = ((slot == rank) & kept).astype(F32)
    return table, jnp.sum(table * weight, axis=1, keepdims=True)


class Stream:
    def __init__(self, sources, slots, sems, block, steps, column, kept=()):
        self.sources, self.slots, self.sems, self.block = sources, slots, sems, block
        self.steps, self.column, self.kept, self.whole = steps, column, kept, sources[0].shape[1] == block

    def copy(self, i, step, keep=False):
        source = self.sources[i]
        if not self.whole:
            source = source.at[:, pl.ds(pl.multiple_of(self.column(step) * self.block, self.block), self.block)]
        slot = lax.rem(step, 2)
        target = self.kept[i] if keep and i < len(self.kept) else self.slots[i].at[slot]
        return pltpu.make_async_copy(source, target, self.sems.at[i, slot])

    def start(self, step, keep=False):
        for i in range(len(self.sources)):
            self.copy(i, step, keep).start()

    def wait(self, i, step, keep=False):
        self.copy(i, step, keep).wait()
        return self.kept[i] if keep and i < len(self.kept) else self.slots[i].at[lax.rem(step, 2)]


def derivatives(x_ref, u_ref, p, block_of_weight):
    x = x_ref[...]
    wg = block_of_weight(0)
    pre_gate = dot(x, wg[...])
    wu = block_of_weight(1)
    pre_up = dot(x, wu[...])
    wd = block_of_weight(2)
    back = dot(u_ref[...], wd[...])
    s = jax.nn.sigmoid(pre_gate)
    activated = pre_gate * s
    hidden = (activated * pre_up).astype(BF)
    scaled_back = p * back
    d_gate = (scaled_back * pre_up * s * (1.0 + pre_gate * (1.0 - s))).astype(BF)
    d_up = (scaled_back * activated).astype(BF)
    return d_gate, d_up, hidden, back, wg, wu


def pieces_of(total, size):
    return [(a, min(size, total - a)) for a in range(0, total, size)]


def own_body(packed, late, steps, groups, cap_ref, routes_ref, tok_hbm, out_hbm, wg_hbm, wu_hbm, wd_hbm, *refs):
    acts_refs, refs = (refs[:4], refs[4:]) if late else (refs[:3], refs[3:])
    kept, refs = (refs[:KEPT], refs[KEPT:]) if late else ((), refs)
    (part_hbm, prob_ref, xq_hbm, sq_hbm, filled_ref, part_ref, xq_ref, sq_ref, tok_ref, out_ref, x_ref, u_ref, p_ref,
     table_ref, acc_ref, wg_ref, wu_ref, wd_ref, sems, row_sems, out_sems) = refs
    step = pl.program_id(0)
    width, block = wg_ref.shape[1:]
    quarter = xq_ref.shape[1]
    stream = Stream((wg_hbm, wu_hbm, wd_hbm), (wg_ref, wu_ref, wd_ref), sems, block, steps, lambda j: j, kept)
    owner, _, group = my_place(part_ref.shape[0])
    half = part_ref.shape[0] // 2
    halves = [pltpu.make_async_copy(part_ref.at[k * half:(k + 1) * half], part_hbm.at[k * half:(k + 1) * half],
                                    out_sems.at[k]) for k in range(2)]
    shares_out = [pltpu.make_async_copy(xq_ref, xq_hbm, out_sems.at[2]),
                  pltpu.make_async_copy(sq_ref, sq_hbm, out_sems.at[3])]

    @pl.when(step == 0)
    def _():
        rows = [pltpu.make_async_copy(tok_hbm, tok_ref, row_sems.at[0]),
                pltpu.make_async_copy(out_hbm, out_ref, row_sems.at[1])]
        rows[0].start()
        stream.copy(0, 0).start()
        rows[1].start()
        stream.copy(1, 0).start()
        stream.copy(2, 0).start()
        table, p = slot_table(routes_ref[...].astype(F32), owner, cap_ref[owner], (group == 1) & (groups == 2))
        table_ref[...] = table.astype(BF)
        p_ref[...] = p
        filled_ref[...] = jnp.sum(table, axis=1, keepdims=True)
        acc_ref[...] = jnp.zeros_like(acc_ref)
        prob_ref[...] = jnp.zeros_like(prob_ref)
        rows[0].wait()
        x_ref[...] = dot(table_ref[...], tok_ref[...]).astype(BF)
        rows[1].wait()
        u_ref[...] = dot(table_ref[...], out_ref[...]).astype(BF)
        at = pl.ds(pl.multiple_of(group * quarter, quarter), quarter)
        xq_ref[...] = x_ref[:, at]
        sq_ref[...] = (p * u_ref[:, at].astype(F32)).astype(BF)
        for copy in shares_out:
            copy.start()

    plain = steps - 1 if late else steps

    @pl.when(step + 1 < plain)
    def _():
        stream.start(step + 1)

    if late:
        @pl.when(step + 1 == plain)
        def _():
            stream.start(step + 1, True)

    def work(keep):
        d_gate, d_up, hidden, back, wg, wu = derivatives(
            x_ref, u_ref, p_ref[...], lambda i: stream.wait(i, step, keep))
        acts = (d_gate, d_up, hidden)

        def store_early():
            for ref, value in zip(acts_refs, acts):
                ref[...] = value

        def store_late():
            for i, value in enumerate(acts):
                acts_refs[3][i] = value

        if keep or not late:
            store_early()
        else:
            pl.when(step >= late)(store_early)
            pl.when(step < late)(store_late)

        prob_ref[...] += jnp.sum(hidden.astype(F32) * back, axis=1, keepdims=True)
        gate_t = d_gate.T
        up_t = d_up.T
        for a, n in pieces_of(width, 512):
            at = slice(a, a + n)
            acc_ref[at, :] += dot(wg[at, :], gate_t) + dot(wu[at, :], up_t)

    @pl.when(step < plain)
    def _():
        work(False)

    if late:
        @pl.when(step == plain)
        def _():
            work(True)

    @pl.when(step == pl.num_programs(0) - 1)
    def _():
        table = table_ref[...]
        count = table.shape[1]
        shares, _, fw = part_ref.shape
        by_slot = (((0,), (1,)), ((), ()))
        if packed:
            total = prob_ref[...]
            high = total.astype(BF).astype(F32)
            lane = lax.broadcasted_iota(jnp.int32, (CAP, 128), 1)
            both = jnp.where(lane == 0, high, jnp.where(lane == 1, total - high, 0.0)).astype(BF)
            by_token = dotg(both, table, FIRST)[:EXTRA].astype(BF)
        for j in range(shares):
            part_ref[j, :count, :] = dotg(table, acc_ref[j * fw:(j + 1) * fw, :].astype(BF), by_slot).astype(BF)
            if packed:
                part_ref[j, count:, :] = jnp.zeros((EXTRA, fw), BF)
                part_ref[j, count:, :count] = by_token
            if (j + 1) % half == 0:
                halves[j // half].start()
        for copy in halves + shares_out:
            copy.wait()


def weight_slots(width, block):
    return [pltpu.VMEM((2, width, block), BF)] * 3 + [pltpu.SemaphoreType.DMA((3, 2))]


def own_group(capacity, routes, tokens, grad_out, wg, wu, wd, shares, groups, packed, block, late):
    count, width = tokens.shape
    hidden = wg.shape[1]
    steps = hidden // block
    tall = count + (EXTRA if packed else 0)
    fw = width // shares
    quarter = width // groups
    act_specs = [pl.BlockSpec((CAP, block), lambda j: (0, jnp.maximum(j - late, 0)))] * 3
    acts = [jax.ShapeDtypeStruct((CAP, (steps - late) * block), BF)] * 3
    if late:
        act_specs.append(pl.BlockSpec((3, CAP, block), lambda j: (0, 0, jnp.minimum(j, late - 1))))
        acts.append(jax.ShapeDtypeStruct((3, CAP, late * block), BF))
        act_specs += [pl.BlockSpec(memory_space=pltpu.VMEM)] * KEPT
        acts += [pltpu.VMEM((width, block), BF)] * KEPT
    column = jax.ShapeDtypeStruct((CAP, 1), F32)
    share = jax.ShapeDtypeStruct((CAP, quarter), BF)
    part = jax.ShapeDtypeStruct((shares, tall, fw), BF)
    rows = pltpu.VMEM((CAP, width), BF)
    tall_rows = pltpu.VMEM((count, width), BF)
    return pl.pallas_call(
        functools.partial(own_body, packed, late, steps, groups),
        grid=(steps,),
        in_specs=[whole_smem(), whole(routes.shape)] + [in_place()] * 5,
        out_specs=act_specs + [in_place(), whole(column.shape), in_place(), in_place(), whole(column.shape)],
        out_shape=acts + [part, column, share, share, column],
        scratch_shapes=[pltpu.VMEM(part.shape, BF)] + [pltpu.VMEM(share.shape, BF)] * 2 + [tall_rows, tall_rows, rows, rows, pltpu.VMEM((CAP, 1), F32), pltpu.VMEM((CAP, count), BF),
                        pltpu.VMEM((width, CAP), F32)] + weight_slots(width, block)
        + [pltpu.SemaphoreType.DMA((2,)), pltpu.SemaphoreType.DMA((4,))],
        compiler_params=params(46),
        cost_estimate=pl.CostEstimate(
            flops=10 * CAP * width * hidden, bytes_accessed=6 * width * hidden, transcendentals=CAP * hidden),
        name="own_group",
    )(capacity, routes, tokens, grad_out, wg, wu, wd)


def joined(mine, other):
    return jnp.concatenate([mine, other], axis=0)


def merged(group, mine, other):
    first, last = jnp.where(group == 0, mine, other), jnp.where(group == 0, other, mine)
    lead = SHORT - CAP
    shared = CAP - lead
    return jnp.concatenate([first[:lead], first[lead:] + last[:shared], last[shared:]], axis=0)


def store_grads(groups, group, fits_ref, xs_ref, ss_ref, mine, other, out_refs):
    def grads(join, rows):
        for i, (rows_ref, out_ref) in enumerate(zip((xs_ref, xs_ref, ss_ref), out_refs)):
            out_ref[...] = dotg(rows_ref[:rows, :], join(mine(i), other(i)), FIRST).astype(BF)

    if groups == 2:
        @pl.when(fits_ref[0] == 1)
        def _():
            grads(functools.partial(merged, group), SHORT)

    @pl.when(fits_ref[0] == 0)
    def _():
        grads(joined, xs_ref.shape[0])


def again_body(groups, shares, steps, late, cap_ref, xq_ref, sq_ref, filled_ref, one_hbm, two_hbm, dg_ref, du_ref, h_ref,
               wg_hbm, wu_hbm, wd_hbm, *refs):
    kept, refs = (refs[:KEPT], refs[KEPT:]) if late else ((), refs)
    (gg_ref, gu_ref, gd_ref, xs_hbm, ss_hbm, fits_ref,
     xs_ref, ss_ref, one_ref, two_ref, xo_ref, uo_ref, po_ref, acts_ref, wg_ref, wu_ref, wd_ref, sems, row_sems) = refs
    step = pl.program_id(0)
    owner, parity, group = my_place(shares)
    quarter = xs_ref.shape[1]
    count = one_ref.shape[1] - EXTRA
    stream = Stream((wg_hbm, wu_hbm, wd_hbm), (wg_ref, wu_ref, wd_ref), sems, wg_ref.shape[2], steps,
                    lambda j: late + lax.rem(j + steps - 1, steps), kept)
    joint = [pltpu.make_async_copy(xs_ref, xs_hbm, row_sems.at[2]), pltpu.make_async_copy(ss_ref, ss_hbm, row_sems.at[3])]

    @pl.when(step == 0)
    def _():
        rows = [pltpu.make_async_copy(one_hbm, one_ref, row_sems.at[0]),
                pltpu.make_async_copy(two_hbm, two_ref, row_sems.at[1])]
        for copy in rows:
            copy.start()
        for i in range(len(kept), 3):
            stream.copy(i, 0).start()
        for copy in rows:
            copy.wait()
        filled = jnp.sum(filled_ref[...])
        for g in range(groups - 1):
            at = slice(g * CAP, (g + 1) * CAP)
            routes = one_ref[g, count:count + EXTRA, :count].astype(F32)
            table, p = slot_table(routes, owner, cap_ref[owner], (group == 0) & (groups == 2))
            filled += jnp.sum(table)
            po_ref[at, :] = p
            table = table.astype(BF)
            from_one = dot(table, one_ref[g, :count, :]).astype(BF)
            from_two = dot(table, two_ref[g, :count, :]).astype(BF)

            @pl.when(parity == 0)
            def _():
                xo_ref[at, :] = from_one
                uo_ref[at, :] = from_two

            @pl.when(parity == 1)
            def _():
                xo_ref[at, :] = from_two
                uo_ref[at, :] = from_one

        fits = filled <= SHORT if groups == 2 else jnp.bool_(False)
        fits_ref[0] = fits.astype(jnp.int32)
        part = pl.ds(pl.multiple_of(group * quarter, quarter), quarter)
        mine, scaled = xq_ref[...], sq_ref[...]
        other = xo_ref[:, part]
        scaled_other = (po_ref[...] * uo_ref[:, part].astype(F32)).astype(BF)
        if groups == 2:
            @pl.when(fits)
            def _():
                xs_ref[:SHORT, :] = merged(group, mine, other)
                ss_ref[:SHORT, :] = merged(group, scaled, scaled_other)

        @pl.when(jnp.logical_not(fits))
        def _():
            xs_ref[...] = joined(mine, other)
            ss_ref[...] = joined(scaled, scaled_other)

        for copy in joint:
            copy.start()

    @pl.when(step + 1 < steps)
    def _():
        stream.start(step + 1)

    def work(keep):
        def block_of_weight(i):
            return kept[i] if keep and i < len(kept) else stream.wait(i, step)

        acts = derivatives(xo_ref, uo_ref, po_ref[...], block_of_weight)
        for i in range(3):
            acts_ref[i] = acts[i]

    if kept:
        @pl.when(step == 0)
        def _():
            work(True)

        @pl.when(step > 0)
        def _():
            work(False)
    else:
        work(False)

    own = (dg_ref, du_ref, h_ref)
    store_grads(groups, group, fits_ref, xs_ref, ss_ref, lambda i: own[i][...], lambda i: acts_ref[i], (gg_ref, gu_ref, gd_ref))

    @pl.when(step == steps - 1)
    def _():
        for copy in joint:
            copy.wait()


def grads_again(capacity, xq, sq, filled, one, two, dg, du, h, wg, wu, wd, kept, groups, shares, block, late):
    width, hidden = wg.shape
    others = (groups - 1) * CAP
    quarter = width // groups
    steps = dg.shape[1] // block
    act = pl.BlockSpec((CAP, block), lambda j: (0, lax.rem(j + steps - 1, steps)))
    grad = pl.BlockSpec((quarter, block), lambda j: (0, late + lax.rem(j + steps - 1, steps)))
    kept = [pltpu.with_memory_space_constraint(w, pltpu.VMEM) for w in kept]
    arrived = pltpu.VMEM(one.shape, BF)
    rows = pltpu.VMEM((others, width), BF)
    joint = jax.ShapeDtypeStruct((CAP + others, quarter), BF)
    return pl.pallas_call(
        functools.partial(again_body, groups, shares, steps, late),
        grid=(steps,),
        in_specs=[whole_smem(), whole(xq.shape), whole(sq.shape), whole(filled.shape), in_place(), in_place(),
                  act, act, act, in_place(), in_place(), in_place()] + [pl.BlockSpec(memory_space=pltpu.VMEM)] * len(kept),
        out_specs=[grad] * 3 + [in_place()] * 2 + [whole_smem()],
        out_shape=[jax.ShapeDtypeStruct((quarter, hidden), BF)] * 3 + [joint] * 2 + [jax.ShapeDtypeStruct((1,), jnp.int32)],
        scratch_shapes=[pltpu.VMEM(joint.shape, BF)] * 2 + [arrived, arrived, rows, rows, pltpu.VMEM((others, 1), F32),
                        pltpu.VMEM((3, others, block), BF)] + weight_slots(width, block) + [pltpu.SemaphoreType.DMA((4,))],
        compiler_params=params(54 if late else 60),
        cost_estimate=pl.CostEstimate(
            flops=(6 * others * width + 6 * (CAP + others) * quarter) * steps * block,
            bytes_accessed=6 * (width + quarter) * steps * block, transcendentals=others * steps * block),
        name="grads_again",
    )(capacity, xq, sq, filled, one, two, dg, du, h, wg, wu, wd, *kept)


def given_body(groups, shares, fits_ref, xs_ref, ss_ref, mine_ref, other_ref, gg_in, gu_in, gd_in, gg_ref, gu_ref, gd_ref):
    _, _, group = my_place(shares)
    store_grads(groups, group, fits_ref, xs_ref, ss_ref, lambda i: mine_ref[i], lambda i: other_ref[i], (gg_ref, gu_ref, gd_ref))


def grads_given(fits, xs, ss, mine, other, grads, groups, shares, block):
    quarter, hidden = grads[0].shape
    steps = mine.shape[2] // block
    grad = pl.BlockSpec((quarter, block), lambda j: (0, j))
    act = pl.BlockSpec((3, CAP, block), lambda j: (0, 0, j))
    return pl.pallas_call(
        functools.partial(given_body, groups, shares),
        grid=(steps,),
        in_specs=[whole_smem(), whole(xs.shape), whole(ss.shape), act, act] + [in_place()] * 3,
        out_specs=[grad] * 3,
        out_shape=[jax.ShapeDtypeStruct((quarter, hidden), BF)] * 3,
        input_output_aliases={5: 0, 6: 1, 7: 2},
        compiler_params=params(),
        cost_estimate=pl.CostEstimate(
            flops=6 * xs.shape[0] * quarter * steps * block, bytes_accessed=6 * quarter * steps * block, transcendentals=0),
        name="grads_given",
    )(fits, xs, ss, mine, other, *grads)


def block_of(hidden, largest):
    for size in (512, 256, 128):
        if size <= largest and hidden % size == 0:
            return size
    return hidden


def per_device(tokens, grad_out, gate_probs, expert_ids, capacity, w_gate, w_up, w_down):
    groups = lax.axis_size("expert")
    shares = lax.axis_size("dp")
    count, width = tokens.shape
    hidden = w_gate.shape[1]
    per_expert = shares // EXPERTS
    packed = width // shares >= count
    block = block_of(hidden, 512)
    steps = hidden // block
    late = steps * 3 // 7 if groups == 2 else 0

    routes, send = pack(expert_ids.T, gate_probs.T, tokens, grad_out, shares)
    arounds = [[(i, (i + shift) % groups) for i in range(groups)] for shift in range(1, groups)]
    one = [lax.ppermute(send, "expert", around) for around in arounds]

    *acts, part, prob, xq, sq, filled = own_group(
        capacity, routes, tokens, grad_out, w_gate, w_up, w_down, shares, groups, packed, block, late)

    one, part = lax.optimization_barrier((one, part))
    swap = [(i, i ^ 1) for i in range(shares)]
    two = [lax.ppermute(rows, "dp", swap) for rows in one]
    acts, kept = acts[:4], acts[4:]
    if late:
        sent = acts.pop()
        sent_other = lax.ppermute(sent, "expert", arounds[0])
    arrived = lax.all_to_all(part, "dp", split_axis=0, concat_axis=0, tiled=True)

    def stacked(parts):
        return parts[0][None] if len(parts) == 1 else jnp.stack(parts)

    *grads, xs, ss, fits = grads_again(
        capacity, xq, sq, filled, stacked(one), stacked(two), *acts, w_gate, w_up, w_down, kept, groups, shares, block, late)
    if late:
        grads = grads_given(fits, xs, ss, sent, sent_other, grads, groups, shares, block)
    grad_gate, grad_up, grad_down = grads

    token_grad = jnp.sum(arrived[:, :count].astype(F32), axis=0).astype(BF)
    if packed:
        ends = arrived[:, count:count + 2, :count].astype(F32)
        by_expert = jnp.sum(ends.reshape(EXPERTS, per_expert * 2, count), axis=1)
    else:
        owner, _, group = my_place(shares)
        table, _ = slot_table(routes.astype(F32), owner, capacity[owner], (group == 1) & (groups == 2))
        mine = jnp.sum(table * prob, axis=0)
        one_hot = (jnp.arange(EXPERTS) == owner).astype(F32)
        by_expert = lax.psum(one_hot[:, None] * mine[None, :], "dp")
    match = expert_ids[:, :, None] == jnp.arange(EXPERTS, dtype=jnp.int32)
    prob_grad = jnp.sum(jnp.where(match, by_expert.T[:, None, :], 0.0), axis=2).astype(BF)
    return (token_grad, prob_grad, grad_gate, grad_up, grad_down)


def solution(mesh):
    return jax.shard_map(
        per_device,
        mesh=mesh,
        in_specs=(
            P("expert", None),
            P("expert", None),
            P("expert", None),
            P("expert", None),
            P(),
            P(None, "dp"),
            P(None, "dp"),
            P(None, "dp"),
        ),
        out_specs=(
            P("expert", "dp"),
            P("expert", None),
            P("expert", "dp"),
            P("expert", "dp"),
            P("expert", "dp"),
        ),
        check_vma=False,
    )
```

```python
import functools

import jax
import jax.numpy as jnp
from jax import lax
from jax.experimental import pallas as pl
from jax.experimental.pallas import tpu as pltpu
from jax.sharding import PartitionSpec as P

EXPERTS = 4
CAP = 144
SHORT = 256
EXTRA = 16
BF = jnp.bfloat16
F32 = jnp.float32
MIB = 1024 * 1024

FIRST = (((0,), (0,)), ((), ()))
LAST = (((1,), (1,)), ((), ()))


def dot(a, b):
    return jnp.dot(a, b, preferred_element_type=F32)


def dotg(a, b, dims):
    return lax.dot_general(a, b, dims, preferred_element_type=F32)


def whole(shape):
    return pl.BlockSpec(shape, lambda *_: (0,) * len(shape), pipeline_mode=pl.Buffered(1))


def params(mib=60):
    return pltpu.CompilerParams(vmem_limit_bytes=mib * MIB)


def whole_smem():
    return pl.BlockSpec(memory_space=pltpu.SMEM)


def in_place():
    return pl.BlockSpec(memory_space=pl.ANY)


def my_place(shares):
    index = lax.axis_index("dp")
    return index // (shares // EXPERTS), index % 2, lax.axis_index("expert")


def pack_body(shares, ids_ref, probs_ref, tok_hbm, out_hbm, routes_ref, send_ref, sem):
    _, parity, _ = my_place(shares)
    count = tok_hbm.shape[0]
    top = send_ref.at[:count]

    @pl.when(parity == 0)
    def _():
        pltpu.make_async_copy(tok_hbm, top, sem).start()

    @pl.when(parity == 1)
    def _():
        pltpu.make_async_copy(out_hbm, top, sem).start()

    ids = ids_ref[...].astype(F32)
    routes = jnp.concatenate([ids, probs_ref[...].astype(F32), jnp.zeros((EXTRA - 4, count), F32)], axis=0).astype(BF)
    routes_ref[...] = routes
    send_ref[count:, :] = jnp.zeros((EXTRA, send_ref.shape[1]), BF)
    send_ref[count:, :count] = routes
    pltpu.make_async_copy(tok_hbm, top, sem).wait()


def pack(ids, probs, tokens, grad_out, shares):
    count, width = tokens.shape
    return pl.pallas_call(
        functools.partial(pack_body, shares),
        in_specs=[whole(ids.shape), whole(probs.shape), in_place(), in_place()],
        out_specs=[whole((EXTRA, count)), whole((count + EXTRA, width))],
        out_shape=[jax.ShapeDtypeStruct((EXTRA, count), BF), jax.ShapeDtypeStruct((count + EXTRA, width), BF)],
        scratch_shapes=[pltpu.SemaphoreType.DMA(())],
        compiler_params=params(16),
        cost_estimate=pl.CostEstimate(flops=0, bytes_accessed=4 * count * width, transcendentals=0),
        name="pack",
    )(ids, probs, tokens, grad_out)


def slot_table(routes, owner, limit, backwards):
    count = routes.shape[1]
    hit = (routes[:2] == owner.astype(F32)).astype(F32)
    named = jnp.sum(hit, axis=0, keepdims=True)
    weight = jnp.sum(hit * routes[2:4], axis=0, keepdims=True)
    row = lax.broadcasted_iota(jnp.int32, (count, count), 0)
    col = lax.broadcasted_iota(jnp.int32, (count, count), 1)
    earlier = (row < col).astype(F32).astype(BF)
    wide = jnp.broadcast_to(named, (16, count)).astype(BF)
    rank = dot(wide, earlier)[:1].astype(jnp.int32)
    kept = (named > 0) & (rank < limit)
    slot = lax.broadcasted_iota(jnp.int32, (CAP, count), 0)
    slot = jnp.where(backwards, CAP - 1 - slot, slot)
    table = ((slot == rank) & kept).astype(F32)
    return table, jnp.sum(table * weight, axis=1, keepdims=True)


class Stream:
    def __init__(self, sources, slots, sems, block, steps):
        self.sources, self.slots, self.sems, self.block = sources, slots, sems, block
        self.steps, self.whole = steps, sources[0].shape[1] == block

    def copy(self, i, step):
        source = self.sources[i]
        if not self.whole:
            source = source.at[:, pl.ds(pl.multiple_of(step * self.block, self.block), self.block)]
        slot = lax.rem(step, 2)
        return pltpu.make_async_copy(source, self.slots[i].at[slot], self.sems.at[i, slot])

    def first(self):
        for i in range(len(self.sources)):
            self.copy(i, 0).start()

    def ahead(self, step):
        @pl.when(step + 1 < self.steps)
        def _():
            for i in range(len(self.sources)):
                self.copy(i, step + 1).start()

    def wait(self, i, step):
        self.copy(i, step).wait()
        return self.slots[i].at[lax.rem(step, 2)]


def derivatives(x_ref, u_ref, p, stream, step):
    x = x_ref[...]
    wg = stream.wait(0, step)
    pre_gate = dot(x, wg[...])
    wu = stream.wait(1, step)
    pre_up = dot(x, wu[...])
    wd = stream.wait(2, step)
    back = dot(u_ref[...], wd[...])
    s = jax.nn.sigmoid(pre_gate)
    activated = pre_gate * s
    hidden = (activated * pre_up).astype(BF)
    scaled_back = p * back
    d_gate = (scaled_back * pre_up * s * (1.0 + pre_gate * (1.0 - s))).astype(BF)
    d_up = (scaled_back * activated).astype(BF)
    return d_gate, d_up, hidden, back, wg, wu


def pieces_of(total, size):
    return [(a, min(size, total - a)) for a in range(0, total, size)]


def own_body(packed, early, groups, cap_ref, routes_ref, tok_hbm, out_hbm, wg_hbm, wu_hbm, wd_hbm, *refs):
    acts_refs, refs = (refs[:3], refs[3:]) if early is None else (refs[:4], refs[4:])
    (part_hbm, prob_ref, xq_hbm, sq_hbm, filled_ref, part_ref, xq_ref, sq_ref, tok_ref, out_ref, x_ref, u_ref, p_ref,
     table_ref, acc_ref, wg_ref, wu_ref, wd_ref, sems, row_sems, out_sems) = refs
    step = pl.program_id(0)
    width, block = wg_ref.shape[1:]
    quarter = xq_ref.shape[1]
    stream = Stream((wg_hbm, wu_hbm, wd_hbm), (wg_ref, wu_ref, wd_ref), sems, block, wg_hbm.shape[1] // block)
    owner, _, group = my_place(part_ref.shape[0])
    half = part_ref.shape[0] // 2
    halves = [pltpu.make_async_copy(part_ref.at[k * half:(k + 1) * half], part_hbm.at[k * half:(k + 1) * half],
                                    out_sems.at[k]) for k in range(2)]
    shares_out = [pltpu.make_async_copy(xq_ref, xq_hbm, out_sems.at[2]),
                  pltpu.make_async_copy(sq_ref, sq_hbm, out_sems.at[3])]

    @pl.when(step == 0)
    def _():
        rows = [pltpu.make_async_copy(tok_hbm, tok_ref, row_sems.at[0]),
                pltpu.make_async_copy(out_hbm, out_ref, row_sems.at[1])]
        rows[0].start()
        stream.copy(0, 0).start()
        rows[1].start()
        stream.copy(1, 0).start()
        stream.copy(2, 0).start()
        table, p = slot_table(routes_ref[...].astype(F32), owner, cap_ref[owner], (group == 1) & (groups == 2))
        table_ref[...] = table.astype(BF)
        p_ref[...] = p
        filled_ref[...] = jnp.sum(table, axis=1, keepdims=True)
        acc_ref[...] = jnp.zeros_like(acc_ref)
        prob_ref[...] = jnp.zeros_like(prob_ref)
        rows[0].wait()
        x_ref[...] = dot(table_ref[...], tok_ref[...]).astype(BF)
        rows[1].wait()
        u_ref[...] = dot(table_ref[...], out_ref[...]).astype(BF)
        at = pl.ds(pl.multiple_of(group * quarter, quarter), quarter)
        xq_ref[...] = x_ref[:, at]
        sq_ref[...] = (p * u_ref[:, at].astype(F32)).astype(BF)
        for copy in shares_out:
            copy.start()

    stream.ahead(step)
    d_gate, d_up, hidden, back, wg, wu = derivatives(x_ref, u_ref, p_ref[...], stream, step)
    acts = (d_gate, d_up, hidden)

    def store_early():
        for ref, value in zip(acts_refs, acts):
            ref[...] = value

    if early is None:
        store_early()
    else:
        pl.when(step < early)(store_early)

        @pl.when(step >= early)
        def _():
            for i, value in enumerate(acts):
                acts_refs[3][i] = value

    prob_ref[...] += jnp.sum(hidden.astype(F32) * back, axis=1, keepdims=True)
    gate_t = d_gate.T
    up_t = d_up.T
    for a, n in pieces_of(width, 512):
        at = slice(a, a + n)
        acc_ref[at, :] += dot(wg[at, :], gate_t) + dot(wu[at, :], up_t)

    @pl.when(step == pl.num_programs(0) - 1)
    def _():
        table = table_ref[...]
        count = table.shape[1]
        shares, _, fw = part_ref.shape
        by_slot = (((0,), (1,)), ((), ()))
        if packed:
            total = prob_ref[...]
            high = total.astype(BF).astype(F32)
            lane = lax.broadcasted_iota(jnp.int32, (CAP, 128), 1)
            both = jnp.where(lane == 0, high, jnp.where(lane == 1, total - high, 0.0)).astype(BF)
            by_token = dotg(both, table, FIRST)[:EXTRA].astype(BF)
        for j in range(shares):
            part_ref[j, :count, :] = dotg(table, acc_ref[j * fw:(j + 1) * fw, :].astype(BF), by_slot).astype(BF)
            if packed:
                part_ref[j, count:, :] = jnp.zeros((EXTRA, fw), BF)
                part_ref[j, count:, :count] = by_token
            if (j + 1) % half == 0:
                halves[j // half].start()
        for copy in halves + shares_out:
            copy.wait()


def weight_slots(width, block):
    return [pltpu.VMEM((2, width, block), BF)] * 3 + [pltpu.SemaphoreType.DMA((3, 2))]


def own_group(capacity, routes, tokens, grad_out, wg, wu, wd, shares, groups, packed, block, early):
    count, width = tokens.shape
    hidden = wg.shape[1]
    steps = hidden // block
    tall = count + (EXTRA if packed else 0)
    fw = width // shares
    quarter = width // groups
    act_specs = [pl.BlockSpec((CAP, block), lambda j: (0, jnp.minimum(j, early - 1)))] * 3
    acts = [jax.ShapeDtypeStruct((CAP, early * block), BF)] * 3
    if early < steps:
        act_specs.append(pl.BlockSpec((3, CAP, block), lambda j: (0, 0, jnp.maximum(j - early, 0))))
        acts.append(jax.ShapeDtypeStruct((3, CAP, (steps - early) * block), BF))
    column = jax.ShapeDtypeStruct((CAP, 1), F32)
    share = jax.ShapeDtypeStruct((CAP, quarter), BF)
    part = jax.ShapeDtypeStruct((shares, tall, fw), BF)
    rows = pltpu.VMEM((CAP, width), BF)
    tall_rows = pltpu.VMEM((count, width), BF)
    return pl.pallas_call(
        functools.partial(own_body, packed, early if early < steps else None, groups),
        grid=(steps,),
        in_specs=[whole_smem(), whole(routes.shape)] + [in_place()] * 5,
        out_specs=act_specs + [in_place(), whole(column.shape), in_place(), in_place(), whole(column.shape)],
        out_shape=acts + [part, column, share, share, column],
        scratch_shapes=[pltpu.VMEM(part.shape, BF)] + [pltpu.VMEM(share.shape, BF)] * 2 + [tall_rows, tall_rows, rows, rows, pltpu.VMEM((CAP, 1), F32), pltpu.VMEM((CAP, count), BF),
                        pltpu.VMEM((width, CAP), F32)] + weight_slots(width, block)
        + [pltpu.SemaphoreType.DMA((2,)), pltpu.SemaphoreType.DMA((4,))],
        compiler_params=params(46),
        cost_estimate=pl.CostEstimate(
            flops=10 * CAP * width * hidden, bytes_accessed=6 * width * hidden, transcendentals=CAP * hidden),
        name="own_group",
    )(capacity, routes, tokens, grad_out, wg, wu, wd)


def joined(mine, other):
    return jnp.concatenate([mine, other], axis=0)


def merged(group, mine, other):
    first, last = jnp.where(group == 0, mine, other), jnp.where(group == 0, other, mine)
    lead = SHORT - CAP
    shared = CAP - lead
    return jnp.concatenate([first[:lead], first[lead:] + last[:shared], last[shared:]], axis=0)


def store_grads(groups, group, fits_ref, xs_ref, ss_ref, mine, other, out_refs):
    def grads(join, rows):
        for i, (rows_ref, out_ref) in enumerate(zip((xs_ref, xs_ref, ss_ref), out_refs)):
            out_ref[...] = dotg(rows_ref[:rows, :], join(mine(i), other(i)), FIRST).astype(BF)

    if groups == 2:
        @pl.when(fits_ref[0] == 1)
        def _():
            grads(functools.partial(merged, group), SHORT)

    @pl.when(fits_ref[0] == 0)
    def _():
        grads(joined, xs_ref.shape[0])


def again_body(groups, shares, steps, cap_ref, xq_ref, sq_ref, filled_ref, one_hbm, two_hbm, dg_ref, du_ref, h_ref,
               wg_hbm, wu_hbm, wd_hbm, gg_ref, gu_ref, gd_ref, xs_hbm, ss_hbm, fits_ref,
               xs_ref, ss_ref, one_ref, two_ref, xo_ref, uo_ref, po_ref, wg_ref, wu_ref, wd_ref, sems, row_sems):
    step = pl.program_id(0)
    owner, parity, group = my_place(shares)
    quarter = xs_ref.shape[1]
    count = one_ref.shape[1] - EXTRA
    stream = Stream((wg_hbm, wu_hbm, wd_hbm), (wg_ref, wu_ref, wd_ref), sems, wg_ref.shape[2], steps)
    joint = [pltpu.make_async_copy(xs_ref, xs_hbm, row_sems.at[2]), pltpu.make_async_copy(ss_ref, ss_hbm, row_sems.at[3])]

    @pl.when(step == 0)
    def _():
        rows = [pltpu.make_async_copy(one_hbm, one_ref, row_sems.at[0]),
                pltpu.make_async_copy(two_hbm, two_ref, row_sems.at[1])]
        for copy in rows:
            copy.start()
        stream.first()
        for copy in rows:
            copy.wait()
        filled = jnp.sum(filled_ref[...])
        for g in range(groups - 1):
            at = slice(g * CAP, (g + 1) * CAP)
            routes = one_ref[g, count:count + EXTRA, :count].astype(F32)
            table, p = slot_table(routes, owner, cap_ref[owner], (group == 0) & (groups == 2))
            filled += jnp.sum(table)
            po_ref[at, :] = p
            table = table.astype(BF)
            from_one = dot(table, one_ref[g, :count, :]).astype(BF)
            from_two = dot(table, two_ref[g, :count, :]).astype(BF)

            @pl.when(parity == 0)
            def _():
                xo_ref[at, :] = from_one
                uo_ref[at, :] = from_two

            @pl.when(parity == 1)
            def _():
                xo_ref[at, :] = from_two
                uo_ref[at, :] = from_one

        fits = filled <= SHORT if groups == 2 else jnp.bool_(False)
        fits_ref[0] = fits.astype(jnp.int32)
        part = pl.ds(pl.multiple_of(group * quarter, quarter), quarter)
        mine, scaled = xq_ref[...], sq_ref[...]
        other = xo_ref[:, part]
        scaled_other = (po_ref[...] * uo_ref[:, part].astype(F32)).astype(BF)
        if groups == 2:
            @pl.when(fits)
            def _():
                xs_ref[:SHORT, :] = merged(group, mine, other)
                ss_ref[:SHORT, :] = merged(group, scaled, scaled_other)

        @pl.when(jnp.logical_not(fits))
        def _():
            xs_ref[...] = joined(mine, other)
            ss_ref[...] = joined(scaled, scaled_other)

        for copy in joint:
            copy.start()

    stream.ahead(step)
    acts = derivatives(xo_ref, uo_ref, po_ref[...], stream, step)
    own = (dg_ref, du_ref, h_ref)
    store_grads(groups, group, fits_ref, xs_ref, ss_ref, lambda i: own[i][...], lambda i: acts[i], (gg_ref, gu_ref, gd_ref))

    @pl.when(step == steps - 1)
    def _():
        for copy in joint:
            copy.wait()


def grads_again(capacity, xq, sq, filled, one, two, dg, du, h, wg, wu, wd, groups, shares, block):
    width, hidden = wg.shape
    others = (groups - 1) * CAP
    quarter = width // groups
    steps = dg.shape[1] // block
    act = pl.BlockSpec((CAP, block), lambda j: (0, j))
    grad = pl.BlockSpec((quarter, block), lambda j: (0, j))
    arrived = pltpu.VMEM(one.shape, BF)
    rows = pltpu.VMEM((others, width), BF)
    joint = jax.ShapeDtypeStruct((CAP + others, quarter), BF)
    return pl.pallas_call(
        functools.partial(again_body, groups, shares, steps),
        grid=(steps,),
        in_specs=[whole_smem(), whole(xq.shape), whole(sq.shape), whole(filled.shape), in_place(), in_place(),
                  act, act, act, in_place(), in_place(), in_place()],
        out_specs=[grad] * 3 + [in_place()] * 2 + [whole_smem()],
        out_shape=[jax.ShapeDtypeStruct((quarter, hidden), BF)] * 3 + [joint] * 2 + [jax.ShapeDtypeStruct((1,), jnp.int32)],
        scratch_shapes=[pltpu.VMEM(joint.shape, BF)] * 2 + [arrived, arrived, rows, rows, pltpu.VMEM((others, 1), F32)]
        + weight_slots(width, block) + [pltpu.SemaphoreType.DMA((4,))],
        compiler_params=params(52 if groups == 2 else 60),
        cost_estimate=pl.CostEstimate(
            flops=(6 * others * width + 6 * (CAP + others) * quarter) * steps * block,
            bytes_accessed=6 * (width + quarter) * steps * block, transcendentals=others * steps * block),
        name="grads_again",
    )(capacity, xq, sq, filled, one, two, dg, du, h, wg, wu, wd)


def given_body(groups, shares, fits_ref, xs_ref, ss_ref, mine_ref, other_ref, gg_in, gu_in, gd_in, gg_ref, gu_ref, gd_ref):
    _, _, group = my_place(shares)
    store_grads(groups, group, fits_ref, xs_ref, ss_ref, lambda i: mine_ref[i], lambda i: other_ref[i], (gg_ref, gu_ref, gd_ref))


def grads_given(fits, xs, ss, mine, other, grads, groups, shares, block):
    quarter, hidden = grads[0].shape
    steps = mine.shape[2] // block
    early = hidden // block - steps
    grad = pl.BlockSpec((quarter, block), lambda j: (0, j + early))
    act = pl.BlockSpec((3, CAP, block), lambda j: (0, 0, j))
    return pl.pallas_call(
        functools.partial(given_body, groups, shares),
        grid=(steps,),
        in_specs=[whole_smem(), whole(xs.shape), whole(ss.shape), act, act] + [in_place()] * 3,
        out_specs=[grad] * 3,
        out_shape=[jax.ShapeDtypeStruct((quarter, hidden), BF)] * 3,
        input_output_aliases={5: 0, 6: 1, 7: 2},
        compiler_params=params(24),
        cost_estimate=pl.CostEstimate(
            flops=6 * xs.shape[0] * quarter * steps * block, bytes_accessed=6 * quarter * steps * block, transcendentals=0),
        name="grads_given",
    )(fits, xs, ss, mine, other, *grads)


def block_of(hidden, largest):
    for size in (512, 256, 128):
        if size <= largest and hidden % size == 0:
            return size
    return hidden


def per_device(tokens, grad_out, gate_probs, expert_ids, capacity, w_gate, w_up, w_down):
    groups = lax.axis_size("expert")
    shares = lax.axis_size("dp")
    count, width = tokens.shape
    hidden = w_gate.shape[1]
    per_expert = shares // EXPERTS
    packed = width // shares >= count
    block = block_of(hidden, 512)
    steps = hidden // block
    early = steps - steps * 3 // 7 if groups == 2 else steps

    routes, send = pack(expert_ids.T, gate_probs.T, tokens, grad_out, shares)
    arounds = [[(i, (i + shift) % groups) for i in range(groups)] for shift in range(1, groups)]
    one = [lax.ppermute(send, "expert", around) for around in arounds]

    *acts, part, prob, xq, sq, filled = own_group(
        capacity, routes, tokens, grad_out, w_gate, w_up, w_down, shares, groups, packed, block, early)

    one, part = lax.optimization_barrier((one, part))
    swap = [(i, i ^ 1) for i in range(shares)]
    two = [lax.ppermute(rows, "dp", swap) for rows in one]
    if early < steps:
        late = acts.pop()
        late_other = lax.ppermute(late, "expert", arounds[0])
    arrived = lax.all_to_all(part, "dp", split_axis=0, concat_axis=0, tiled=True)

    def stacked(parts):
        return parts[0][None] if len(parts) == 1 else jnp.stack(parts)

    *grads, xs, ss, fits = grads_again(
        capacity, xq, sq, filled, stacked(one), stacked(two), *acts, w_gate, w_up, w_down, groups, shares, block)
    if early < steps:
        grads = grads_given(fits, xs, ss, late, late_other, grads, groups, shares, block_of(late.shape[2], 256))
    grad_gate, grad_up, grad_down = grads

    token_grad = jnp.sum(arrived[:, :count].astype(F32), axis=0).astype(BF)
    if packed:
        ends = arrived[:, count:count + 2, :count].astype(F32)
        by_expert = jnp.sum(ends.reshape(EXPERTS, per_expert * 2, count), axis=1)
    else:
        owner, _, group = my_place(shares)
        table, _ = slot_table(routes.astype(F32), owner, capacity[owner], (group == 1) & (groups == 2))
        mine = jnp.sum(table * prob, axis=0)
        one_hot = (jnp.arange(EXPERTS) == owner).astype(F32)
        by_expert = lax.psum(one_hot[:, None] * mine[None, :], "dp")
    match = expert_ids[:, :, None] == jnp.arange(EXPERTS, dtype=jnp.int32)
    prob_grad = jnp.sum(jnp.where(match, by_expert.T[:, None, :], 0.0), axis=2).astype(BF)
    return (token_grad, prob_grad, grad_gate, grad_up, grad_down)


def solution(mesh):
    return jax.shard_map(
        per_device,
        mesh=mesh,
        in_specs=(
            P("expert", None),
            P("expert", None),
            P("expert", None),
            P("expert", None),
            P(),
            P(None, "dp"),
            P(None, "dp"),
            P(None, "dp"),
        ),
        out_specs=(
            P("expert", "dp"),
            P("expert", None),
            P("expert", "dp"),
            P("expert", "dp"),
            P("expert", "dp"),
        ),
        check_vma=False,
    )
```

```python
import functools

import jax
import jax.numpy as jnp
from jax import lax
from jax.experimental import pallas as pl
from jax.experimental.pallas import tpu as pltpu
from jax.sharding import PartitionSpec as P

EXPERTS = 4
CAP = 144
SHORT = 256
EXTRA = 16
BF = jnp.bfloat16
F32 = jnp.float32
VMEM_LIMIT = 60 * 1024 * 1024

FIRST = (((0,), (0,)), ((), ()))
LAST = (((1,), (1,)), ((), ()))


def dot(a, b):
    return jnp.dot(a, b, preferred_element_type=F32)


def dotg(a, b, dims):
    return lax.dot_general(a, b, dims, preferred_element_type=F32)


def whole(shape):
    return pl.BlockSpec(shape, lambda *_: (0,) * len(shape), pipeline_mode=pl.Buffered(1))


def params():
    return pltpu.CompilerParams(vmem_limit_bytes=VMEM_LIMIT)


def whole_smem():
    return pl.BlockSpec(memory_space=pltpu.SMEM)


def in_place():
    return pl.BlockSpec(memory_space=pl.ANY)


def my_place(shares):
    index = lax.axis_index("dp")
    return index // (shares // EXPERTS), index % 2, lax.axis_index("expert")


def pack_body(shares, ids_hbm, probs_hbm, tok_hbm, out_hbm, routes_hbm, send_hbm, ids_ref, probs_ref, routes_ref, rows_ref,
              in_sems, out_sems):
    _, parity, _ = my_place(shares)
    count = tok_hbm.shape[0]
    half = count // 2
    tops = [slice(0, half), slice(half, count)]
    small = [pltpu.make_async_copy(ids_hbm, ids_ref, in_sems.at[2]), pltpu.make_async_copy(probs_hbm, probs_ref, in_sems.at[3])]
    for copy in small:
        copy.start()

    def arrival(rows_hbm, k):
        return pltpu.make_async_copy(rows_hbm.at[tops[k]], rows_ref.at[tops[k]], in_sems.at[k])

    for value, rows_hbm in enumerate((tok_hbm, out_hbm)):
        @pl.when(parity == value)
        def _():
            for k in range(2):
                arrival(rows_hbm, k).start()

    for copy in small:
        copy.wait()
    ids = ids_ref[...].astype(F32)
    routes = jnp.concatenate([ids, probs_ref[...].astype(F32), jnp.zeros((EXTRA - 4, count), F32)], axis=0).astype(BF)
    routes_ref[...] = routes
    rows_ref[count:, :] = jnp.zeros((EXTRA, rows_ref.shape[1]), BF)
    rows_ref[count:, :count] = routes
    below = slice(count, count + EXTRA)
    leaving = [pltpu.make_async_copy(rows_ref.at[at], send_hbm.at[at], out_sems.at[k]) for k, at in enumerate(tops + [below])]
    leaving.append(pltpu.make_async_copy(routes_ref, routes_hbm, out_sems.at[3]))
    leaving[2].start()
    leaving[3].start()
    for k in range(2):
        arrival(tok_hbm, k).wait()
        leaving[k].start()
    for copy in leaving:
        copy.wait()


def pack(ids, probs, tokens, grad_out, shares):
    count, width = tokens.shape
    return pl.pallas_call(
        functools.partial(pack_body, shares),
        in_specs=[in_place()] * 4,
        out_specs=[in_place()] * 2,
        out_shape=[jax.ShapeDtypeStruct((EXTRA, count), BF), jax.ShapeDtypeStruct((count + EXTRA, width), BF)],
        scratch_shapes=[pltpu.VMEM(ids.shape, ids.dtype), pltpu.VMEM(probs.shape, BF), pltpu.VMEM((EXTRA, count), BF),
                        pltpu.VMEM((count + EXTRA, width), BF), pltpu.SemaphoreType.DMA((4,)), pltpu.SemaphoreType.DMA((4,))],
        compiler_params=params(),
        cost_estimate=pl.CostEstimate(flops=0, bytes_accessed=4 * count * width, transcendentals=0),
        name="pack",
    )(ids, probs, tokens, grad_out)


def slot_table(routes, owner, limit, backwards):
    count = routes.shape[1]
    hit = (routes[:2] == owner.astype(F32)).astype(F32)
    named = jnp.sum(hit, axis=0, keepdims=True)
    weight = jnp.sum(hit * routes[2:4], axis=0, keepdims=True)
    row = lax.broadcasted_iota(jnp.int32, (count, count), 0)
    col = lax.broadcasted_iota(jnp.int32, (count, count), 1)
    earlier = (row < col).astype(F32).astype(BF)
    wide = jnp.broadcast_to(named, (16, count)).astype(BF)
    rank = dot(wide, earlier)[:1].astype(jnp.int32)
    kept = (named > 0) & (rank < limit)
    slot = lax.broadcasted_iota(jnp.int32, (CAP, count), 0)
    slot = jnp.where(backwards, CAP - 1 - slot, slot)
    table = ((slot == rank) & kept).astype(F32)
    return table, jnp.sum(table * weight, axis=1, keepdims=True)


class Stream:
    def __init__(self, sources, slots, sems, block, steps):
        self.sources, self.slots, self.sems, self.block = sources, slots, sems, block
        self.steps, self.whole = steps, sources[0].shape[1] == block

    def copy(self, i, step):
        source = self.sources[i]
        if not self.whole:
            source = source.at[:, pl.ds(pl.multiple_of(step * self.block, self.block), self.block)]
        slot = lax.rem(step, 2)
        return pltpu.make_async_copy(source, self.slots[i].at[slot], self.sems.at[i, slot])

    def first(self):
        for i in range(len(self.sources)):
            self.copy(i, 0).start()

    def ahead(self, step):
        @pl.when(step + 1 < self.steps)
        def _():
            for i in range(len(self.sources)):
                self.copy(i, step + 1).start()

    def wait(self, i, step):
        self.copy(i, step).wait()
        return self.slots[i].at[lax.rem(step, 2)]


def derivatives(x_ref, u_ref, p, stream, step):
    x = x_ref[...]
    wg = stream.wait(0, step)
    pre_gate = dot(x, wg[...])
    wu = stream.wait(1, step)
    pre_up = dot(x, wu[...])
    wd = stream.wait(2, step)
    back = dot(u_ref[...], wd[...])
    s = jax.nn.sigmoid(pre_gate)
    activated = pre_gate * s
    hidden = (activated * pre_up).astype(BF)
    scaled_back = p * back
    d_gate = (scaled_back * pre_up * s * (1.0 + pre_gate * (1.0 - s))).astype(BF)
    d_up = (scaled_back * activated).astype(BF)
    return d_gate, d_up, hidden, back, wg, wu


def pieces_of(total, size):
    return [(a, min(size, total - a)) for a in range(0, total, size)]


def own_body(packed, early, groups, cap_ref, routes_hbm, tok_hbm, out_hbm, wg_hbm, wu_hbm, wd_hbm, *refs):
    acts_refs, refs = (refs[:3], refs[3:]) if early is None else (refs[:4], refs[4:])
    (part_hbm, prob_ref, xq_hbm, sq_hbm, filled_ref, part_ref, xq_ref, sq_ref, routes_ref, tok_ref, out_ref, x_ref, u_ref, p_ref,
     table_ref, acc_ref, wg_ref, wu_ref, wd_ref, sems, row_sems, out_sems) = refs
    step = pl.program_id(0)
    width, block = wg_ref.shape[1:]
    quarter = xq_ref.shape[1]
    stream = Stream((wg_hbm, wu_hbm, wd_hbm), (wg_ref, wu_ref, wd_ref), sems, block, wg_hbm.shape[1] // block)
    owner, _, group = my_place(part_ref.shape[0])
    half = part_ref.shape[0] // 2
    halves = [pltpu.make_async_copy(part_ref.at[k * half:(k + 1) * half], part_hbm.at[k * half:(k + 1) * half],
                                    out_sems.at[k]) for k in range(2)]
    shares_out = [pltpu.make_async_copy(xq_ref, xq_hbm, out_sems.at[2]),
                  pltpu.make_async_copy(sq_ref, sq_hbm, out_sems.at[3])]

    @pl.when(step == 0)
    def _():
        rows = [pltpu.make_async_copy(tok_hbm, tok_ref, row_sems.at[0]),
                pltpu.make_async_copy(out_hbm, out_ref, row_sems.at[1]),
                pltpu.make_async_copy(routes_hbm, routes_ref, row_sems.at[2])]
        rows[2].start()
        rows[0].start()
        stream.copy(0, 0).start()
        rows[1].start()
        stream.copy(1, 0).start()
        stream.copy(2, 0).start()
        acc_ref[...] = jnp.zeros_like(acc_ref)
        prob_ref[...] = jnp.zeros_like(prob_ref)
        rows[2].wait()
        table, p = slot_table(routes_ref[...].astype(F32), owner, cap_ref[owner], (group == 1) & (groups == 2))
        table_ref[...] = table.astype(BF)
        p_ref[...] = p
        filled_ref[...] = jnp.sum(table, axis=1, keepdims=True)
        rows[0].wait()
        x_ref[...] = dot(table_ref[...], tok_ref[...]).astype(BF)
        rows[1].wait()
        u_ref[...] = dot(table_ref[...], out_ref[...]).astype(BF)
        at = pl.ds(pl.multiple_of(group * quarter, quarter), quarter)
        xq_ref[...] = x_ref[:, at]
        sq_ref[...] = (p * u_ref[:, at].astype(F32)).astype(BF)
        for copy in shares_out:
            copy.start()

    stream.ahead(step)
    d_gate, d_up, hidden, back, wg, wu = derivatives(x_ref, u_ref, p_ref[...], stream, step)
    acts = (d_gate, d_up, hidden)

    def store_early():
        for ref, value in zip(acts_refs, acts):
            ref[...] = value

    if early is None:
        store_early()
    else:
        pl.when(step < early)(store_early)

        @pl.when(step >= early)
        def _():
            for i, value in enumerate(acts):
                acts_refs[3][i] = value

    prob_ref[...] += jnp.sum(hidden.astype(F32) * back, axis=1, keepdims=True)
    gate_t = d_gate.T
    up_t = d_up.T
    for a, n in pieces_of(width, 512):
        at = slice(a, a + n)
        acc_ref[at, :] += dot(wg[at, :], gate_t) + dot(wu[at, :], up_t)

    @pl.when(step == pl.num_programs(0) - 1)
    def _():
        table = table_ref[...]
        count = table.shape[1]
        shares, _, fw = part_ref.shape
        by_slot = (((0,), (1,)), ((), ()))
        if packed:
            total = prob_ref[...]
            high = total.astype(BF).astype(F32)
            lane = lax.broadcasted_iota(jnp.int32, (CAP, 128), 1)
            both = jnp.where(lane == 0, high, jnp.where(lane == 1, total - high, 0.0)).astype(BF)
            by_token = dotg(both, table, FIRST)[:EXTRA].astype(BF)
        for j in range(shares):
            part_ref[j, :count, :] = dotg(table, acc_ref[j * fw:(j + 1) * fw, :].astype(BF), by_slot).astype(BF)
            if packed:
                part_ref[j, count:, :] = jnp.zeros((EXTRA, fw), BF)
                part_ref[j, count:, :count] = by_token
            if (j + 1) % half == 0:
                halves[j // half].start()
        for copy in halves + shares_out:
            copy.wait()


def weight_slots(width, block, copied=3):
    return [pltpu.VMEM((2, width, block), BF)] * 3 + [pltpu.SemaphoreType.DMA((copied, 2))]


def own_group(capacity, routes, tokens, grad_out, wg, wu, wd, shares, groups, packed, block, early):
    count, width = tokens.shape
    hidden = wg.shape[1]
    steps = hidden // block
    tall = count + (EXTRA if packed else 0)
    fw = width // shares
    quarter = width // groups
    act_specs = [pl.BlockSpec((CAP, block), lambda j: (0, jnp.minimum(j, early - 1)))] * 3
    acts = [jax.ShapeDtypeStruct((CAP, early * block), BF)] * 3
    if early < steps:
        act_specs.append(pl.BlockSpec((3, CAP, block), lambda j: (0, 0, jnp.maximum(j - early, 0))))
        acts.append(jax.ShapeDtypeStruct((3, CAP, (steps - early) * block), BF))
    column = jax.ShapeDtypeStruct((CAP, 1), F32)
    share = jax.ShapeDtypeStruct((CAP, quarter), BF)
    part = jax.ShapeDtypeStruct((shares, tall, fw), BF)
    rows = pltpu.VMEM((CAP, width), BF)
    tall_rows = pltpu.VMEM((count, width), BF)
    return pl.pallas_call(
        functools.partial(own_body, packed, early if early < steps else None, groups),
        grid=(steps,),
        in_specs=[whole_smem()] + [in_place()] * 6,
        out_specs=act_specs + [in_place(), whole(column.shape), in_place(), in_place(), whole(column.shape)],
        out_shape=acts + [part, column, share, share, column],
        scratch_shapes=[pltpu.VMEM(part.shape, BF)] + [pltpu.VMEM(share.shape, BF)] * 2 + [pltpu.VMEM(routes.shape, BF), tall_rows, tall_rows, rows, rows, pltpu.VMEM((CAP, 1), F32), pltpu.VMEM((CAP, count), BF),
                        pltpu.VMEM((width, CAP), F32)] + weight_slots(width, block)
        + [pltpu.SemaphoreType.DMA((3,)), pltpu.SemaphoreType.DMA((4,))],
        compiler_params=params(),
        cost_estimate=pl.CostEstimate(
            flops=10 * CAP * width * hidden, bytes_accessed=6 * width * hidden, transcendentals=CAP * hidden),
        name="own_group",
    )(capacity, routes, tokens, grad_out, wg, wu, wd)


def joined(mine, other):
    return jnp.concatenate([mine, other], axis=0)


def merged(group, mine, other):
    first, last = jnp.where(group == 0, mine, other), jnp.where(group == 0, other, mine)
    lead = SHORT - CAP
    shared = CAP - lead
    return jnp.concatenate([first[:lead], first[lead:] + last[:shared], last[shared:]], axis=0)


def store_grads(groups, group, fits_ref, xs_ref, ss_ref, mine, other, out_refs):
    def grads(join, rows):
        for i, (rows_ref, out_ref) in enumerate(zip((xs_ref, xs_ref, ss_ref), out_refs)):
            out_ref[...] = dotg(rows_ref[:rows, :], join(mine(i), other(i)), FIRST).astype(BF)

    if groups == 2:
        @pl.when(fits_ref[0] == 1)
        def _():
            grads(functools.partial(merged, group), SHORT)

    @pl.when(fits_ref[0] == 0)
    def _():
        grads(joined, xs_ref.shape[0])


def again_body(groups, shares, steps, cap_ref, xq_hbm, sq_hbm, filled_hbm, one_hbm, two_hbm, dg_hbm, du_hbm, h_hbm,
               wg_hbm, wu_hbm, wd_hbm, gg_ref, gu_ref, gd_ref, xs_hbm, ss_hbm, fits_ref,
               xq_ref, sq_ref, filled_ref, dg_ref, du_ref, h_ref, xs_ref, ss_ref, one_ref, two_ref, xo_ref, uo_ref, po_ref, wg_ref, wu_ref, wd_ref, sems, row_sems):
    step = pl.program_id(0)
    owner, parity, group = my_place(shares)
    quarter = xs_ref.shape[1]
    count = one_ref.shape[1] - EXTRA
    stream = Stream((wg_hbm, wu_hbm, wd_hbm, dg_hbm, du_hbm, h_hbm), (wg_ref, wu_ref, wd_ref, dg_ref, du_ref, h_ref), sems,
                    wg_ref.shape[2], steps)
    joint = [pltpu.make_async_copy(xs_ref, xs_hbm, row_sems.at[2]), pltpu.make_async_copy(ss_ref, ss_hbm, row_sems.at[3])]

    @pl.when(step == 0)
    def _():
        rows = [pltpu.make_async_copy(one_hbm, one_ref, row_sems.at[0]),
                pltpu.make_async_copy(two_hbm, two_ref, row_sems.at[1]),
                pltpu.make_async_copy(filled_hbm, filled_ref, row_sems.at[4]),
                pltpu.make_async_copy(xq_hbm, xq_ref, row_sems.at[5]),
                pltpu.make_async_copy(sq_hbm, sq_ref, row_sems.at[6])]
        for copy in rows:
            copy.start()
        stream.first()
        for copy in rows:
            copy.wait()
        filled = jnp.sum(filled_ref[...])
        for g in range(groups - 1):
            at = slice(g * CAP, (g + 1) * CAP)
            routes = one_ref[g, count:count + EXTRA, :count].astype(F32)
            table, p = slot_table(routes, owner, cap_ref[owner], (group == 0) & (groups == 2))
            filled += jnp.sum(table)
            po_ref[at, :] = p
            table = table.astype(BF)
            from_one = dot(table, one_ref[g, :count, :]).astype(BF)
            from_two = dot(table, two_ref[g, :count, :]).astype(BF)

            @pl.when(parity == 0)
            def _():
                xo_ref[at, :] = from_one
                uo_ref[at, :] = from_two

            @pl.when(parity == 1)
            def _():
                xo_ref[at, :] = from_two
                uo_ref[at, :] = from_one

        fits = filled <= SHORT if groups == 2 else jnp.bool_(False)
        fits_ref[0] = fits.astype(jnp.int32)
        part = pl.ds(pl.multiple_of(group * quarter, quarter), quarter)
        mine, scaled = xq_ref[...], sq_ref[...]
        other = xo_ref[:, part]
        scaled_other = (po_ref[...] * uo_ref[:, part].astype(F32)).astype(BF)
        if groups == 2:
            @pl.when(fits)
            def _():
                xs_ref[:SHORT, :] = merged(group, mine, other)
                ss_ref[:SHORT, :] = merged(group, scaled, scaled_other)

        @pl.when(jnp.logical_not(fits))
        def _():
            xs_ref[...] = joined(mine, other)
            ss_ref[...] = joined(scaled, scaled_other)

        for copy in joint:
            copy.start()

    stream.ahead(step)
    acts = derivatives(xo_ref, uo_ref, po_ref[...], stream, step)
    own = [stream.wait(3 + i, step) for i in range(3)]
    store_grads(groups, group, fits_ref, xs_ref, ss_ref, lambda i: own[i][...], lambda i: acts[i], (gg_ref, gu_ref, gd_ref))

    @pl.when(step == steps - 1)
    def _():
        for copy in joint:
            copy.wait()


def grads_again(capacity, xq, sq, filled, one, two, dg, du, h, wg, wu, wd, groups, shares, block):
    width, hidden = wg.shape
    others = (groups - 1) * CAP
    quarter = width // groups
    steps = dg.shape[1] // block
    act = pltpu.VMEM((2, CAP, block), BF)
    grad = pl.BlockSpec((quarter, block), lambda j: (0, j))
    arrived = pltpu.VMEM(one.shape, BF)
    rows = pltpu.VMEM((others, width), BF)
    joint = jax.ShapeDtypeStruct((CAP + others, quarter), BF)
    return pl.pallas_call(
        functools.partial(again_body, groups, shares, steps),
        grid=(steps,),
        in_specs=[whole_smem()] + [in_place()] * 11,
        out_specs=[grad] * 3 + [in_place()] * 2 + [whole_smem()],
        out_shape=[jax.ShapeDtypeStruct((quarter, hidden), BF)] * 3 + [joint] * 2 + [jax.ShapeDtypeStruct((1,), jnp.int32)],
        scratch_shapes=[pltpu.VMEM(xq.shape, BF), pltpu.VMEM(sq.shape, BF), pltpu.VMEM(filled.shape, F32), act, act, act]
        + [pltpu.VMEM(joint.shape, BF)] * 2 + [arrived, arrived, rows, rows, pltpu.VMEM((others, 1), F32)]
        + weight_slots(width, block, 6) + [pltpu.SemaphoreType.DMA((7,))],
        compiler_params=params(),
        cost_estimate=pl.CostEstimate(
            flops=(6 * others * width + 6 * (CAP + others) * quarter) * steps * block,
            bytes_accessed=6 * (width + quarter) * steps * block, transcendentals=others * steps * block),
        name="grads_again",
    )(capacity, xq, sq, filled, one, two, dg, du, h, wg, wu, wd)


def given_body(groups, shares, fits_ref, xs_ref, ss_ref, mine_ref, other_ref, gg_in, gu_in, gd_in, gg_ref, gu_ref, gd_ref):
    _, _, group = my_place(shares)
    store_grads(groups, group, fits_ref, xs_ref, ss_ref, lambda i: mine_ref[i], lambda i: other_ref[i], (gg_ref, gu_ref, gd_ref))


def grads_given(fits, xs, ss, mine, other, grads, groups, shares, block):
    quarter, hidden = grads[0].shape
    steps = mine.shape[2] // block
    early = hidden // block - steps
    grad = pl.BlockSpec((quarter, block), lambda j: (0, j + early))
    act = pl.BlockSpec((3, CAP, block), lambda j: (0, 0, j))
    return pl.pallas_call(
        functools.partial(given_body, groups, shares),
        grid=(steps,),
        in_specs=[whole_smem(), whole(xs.shape), whole(ss.shape), act, act] + [in_place()] * 3,
        out_specs=[grad] * 3,
        out_shape=[jax.ShapeDtypeStruct((quarter, hidden), BF)] * 3,
        input_output_aliases={5: 0, 6: 1, 7: 2},
        compiler_params=params(),
        cost_estimate=pl.CostEstimate(
            flops=6 * xs.shape[0] * quarter * steps * block, bytes_accessed=6 * quarter * steps * block, transcendentals=0),
        name="grads_given",
    )(fits, xs, ss, mine, other, *grads)


def block_of(hidden, largest):
    for size in (512, 256, 128):
        if size <= largest and hidden % size == 0:
            return size
    return hidden


def per_device(tokens, grad_out, gate_probs, expert_ids, capacity, w_gate, w_up, w_down):
    groups = lax.axis_size("expert")
    shares = lax.axis_size("dp")
    count, width = tokens.shape
    hidden = w_gate.shape[1]
    per_expert = shares // EXPERTS
    packed = width // shares >= count
    block = block_of(hidden, 512)
    steps = hidden // block
    early = steps - steps * 3 // 7 if groups == 2 else steps

    routes, send = pack(expert_ids.T, gate_probs.T, tokens, grad_out, shares)
    arounds = [[(i, (i + shift) % groups) for i in range(groups)] for shift in range(1, groups)]
    one = [lax.ppermute(send, "expert", around) for around in arounds]

    *acts, part, prob, xq, sq, filled = own_group(
        capacity, routes, tokens, grad_out, w_gate, w_up, w_down, shares, groups, packed, block, early)

    one, part = lax.optimization_barrier((one, part))
    swap = [(i, i ^ 1) for i in range(shares)]
    two = [lax.ppermute(rows, "dp", swap) for rows in one]
    if early < steps:
        late = acts.pop()
        late_other = lax.ppermute(late, "expert", arounds[0])
    arrived = lax.all_to_all(part, "dp", split_axis=0, concat_axis=0, tiled=True)

    def stacked(parts):
        return parts[0][None] if len(parts) == 1 else jnp.stack(parts)

    *grads, xs, ss, fits = grads_again(
        capacity, xq, sq, filled, stacked(one), stacked(two), *acts, w_gate, w_up, w_down, groups, shares, block)
    if early < steps:
        grads = grads_given(fits, xs, ss, late, late_other, grads, groups, shares, block_of(late.shape[2], 256))
    grad_gate, grad_up, grad_down = grads

    token_grad = jnp.sum(arrived[:, :count].astype(F32), axis=0).astype(BF)
    if packed:
        ends = arrived[:, count:count + 2, :count].astype(F32)
        by_expert = jnp.sum(ends.reshape(EXPERTS, per_expert * 2, count), axis=1)
    else:
        owner, _, group = my_place(shares)
        table, _ = slot_table(routes.astype(F32), owner, capacity[owner], (group == 1) & (groups == 2))
        mine = jnp.sum(table * prob, axis=0)
        one_hot = (jnp.arange(EXPERTS) == owner).astype(F32)
        by_expert = lax.psum(one_hot[:, None] * mine[None, :], "dp")
    match = expert_ids[:, :, None] == jnp.arange(EXPERTS, dtype=jnp.int32)
    prob_grad = jnp.sum(jnp.where(match, by_expert.T[:, None, :], 0.0), axis=2).astype(BF)
    return (token_grad, prob_grad, grad_gate, grad_up, grad_down)


def solution(mesh):
    return jax.shard_map(
        per_device,
        mesh=mesh,
        in_specs=(
            P("expert", None),
            P("expert", None),
            P("expert", None),
            P("expert", None),
            P(),
            P(None, "dp"),
            P(None, "dp"),
            P(None, "dp"),
        ),
        out_specs=(
            P("expert", "dp"),
            P("expert", None),
            P("expert", "dp"),
            P("expert", "dp"),
            P("expert", "dp"),
        ),
        check_vma=False,
    )
```

```python
import functools

import jax
import jax.numpy as jnp
from jax import lax
from jax.experimental import pallas as pl
from jax.experimental.pallas import tpu as pltpu
from jax.sharding import PartitionSpec as P

EXPERTS = 4
CAP = 144
SHORT = 256
EXTRA = 16
BF = jnp.bfloat16
F32 = jnp.float32
MIB = 1024 * 1024

FIRST = (((0,), (0,)), ((), ()))
LAST = (((1,), (1,)), ((), ()))


def dot(a, b):
    return jnp.dot(a, b, preferred_element_type=F32)


def dotg(a, b, dims):
    return lax.dot_general(a, b, dims, preferred_element_type=F32)


def whole(shape):
    return pl.BlockSpec(shape, lambda *_: (0,) * len(shape), pipeline_mode=pl.Buffered(1))


def params(mib=60):
    return pltpu.CompilerParams(vmem_limit_bytes=mib * MIB)


def whole_smem():
    return pl.BlockSpec(memory_space=pltpu.SMEM)


def in_place():
    return pl.BlockSpec(memory_space=pl.ANY)


def my_place(shares):
    index = lax.axis_index("dp")
    return index // (shares // EXPERTS), index % 2, lax.axis_index("expert")


def pack_body(shares, ids_hbm, probs_hbm, tok_hbm, out_hbm, routes_hbm, send_hbm, ids_ref, probs_ref, routes_ref, rows_ref,
              in_sems, out_sems):
    _, parity, _ = my_place(shares)
    count = tok_hbm.shape[0]
    half = count // 2
    tops = [slice(0, half), slice(half, count)]
    small = [pltpu.make_async_copy(ids_hbm, ids_ref, in_sems.at[2]), pltpu.make_async_copy(probs_hbm, probs_ref, in_sems.at[3])]
    for copy in small:
        copy.start()

    def arrival(rows_hbm, k):
        return pltpu.make_async_copy(rows_hbm.at[tops[k]], rows_ref.at[tops[k]], in_sems.at[k])

    for value, rows_hbm in enumerate((tok_hbm, out_hbm)):
        @pl.when(parity == value)
        def _():
            for k in range(2):
                arrival(rows_hbm, k).start()

    for copy in small:
        copy.wait()
    ids = ids_ref[...].astype(F32)
    routes = jnp.concatenate([ids, probs_ref[...].astype(F32), jnp.zeros((EXTRA - 4, count), F32)], axis=0).astype(BF)
    routes_ref[...] = routes
    rows_ref[count:, :] = jnp.zeros((EXTRA, rows_ref.shape[1]), BF)
    rows_ref[count:, :count] = routes
    below = slice(count, count + EXTRA)
    leaving = [pltpu.make_async_copy(rows_ref.at[at], send_hbm.at[at], out_sems.at[k]) for k, at in enumerate(tops + [below])]
    leaving.append(pltpu.make_async_copy(routes_ref, routes_hbm, out_sems.at[3]))
    leaving[2].start()
    leaving[3].start()
    for k in range(2):
        arrival(tok_hbm, k).wait()
        leaving[k].start()
    for copy in leaving:
        copy.wait()


def pack(ids, probs, tokens, grad_out, shares):
    count, width = tokens.shape
    return pl.pallas_call(
        functools.partial(pack_body, shares),
        in_specs=[in_place()] * 4,
        out_specs=[in_place()] * 2,
        out_shape=[jax.ShapeDtypeStruct((EXTRA, count), BF), jax.ShapeDtypeStruct((count + EXTRA, width), BF)],
        scratch_shapes=[pltpu.VMEM(ids.shape, ids.dtype), pltpu.VMEM(probs.shape, BF), pltpu.VMEM((EXTRA, count), BF),
                        pltpu.VMEM((count + EXTRA, width), BF), pltpu.SemaphoreType.DMA((4,)), pltpu.SemaphoreType.DMA((4,))],
        compiler_params=params(),
        cost_estimate=pl.CostEstimate(flops=0, bytes_accessed=4 * count * width, transcendentals=0),
        name="pack",
    )(ids, probs, tokens, grad_out)


def slot_table(routes, owner, limit, backwards):
    count = routes.shape[1]
    hit = (routes[:2] == owner.astype(F32)).astype(F32)
    named = jnp.sum(hit, axis=0, keepdims=True)
    weight = jnp.sum(hit * routes[2:4], axis=0, keepdims=True)
    row = lax.broadcasted_iota(jnp.int32, (count, count), 0)
    col = lax.broadcasted_iota(jnp.int32, (count, count), 1)
    earlier = (row < col).astype(F32).astype(BF)
    wide = jnp.broadcast_to(named, (16, count)).astype(BF)
    rank = dot(wide, earlier)[:1].astype(jnp.int32)
    kept = (named > 0) & (rank < limit)
    slot = lax.broadcasted_iota(jnp.int32, (CAP, count), 0)
    slot = jnp.where(backwards, CAP - 1 - slot, slot)
    table = ((slot == rank) & kept).astype(F32)
    return table, jnp.sum(table * weight, axis=1, keepdims=True)


class Stream:
    def __init__(self, sources, slots, sems, block, steps):
        self.sources, self.slots, self.sems, self.block = sources, slots, sems, block
        self.steps, self.whole = steps, sources[0].shape[1] == block

    def copy(self, i, step):
        source = self.sources[i]
        if not self.whole:
            source = source.at[:, pl.ds(pl.multiple_of(step * self.block, self.block), self.block)]
        slot = lax.rem(step, 2)
        return pltpu.make_async_copy(source, self.slots[i].at[slot], self.sems.at[i, slot])

    def first(self):
        for i in range(len(self.sources)):
            self.copy(i, 0).start()

    def ahead(self, step):
        @pl.when(step + 1 < self.steps)
        def _():
            for i in range(len(self.sources)):
                self.copy(i, step + 1).start()

    def wait(self, i, step):
        self.copy(i, step).wait()
        return self.slots[i].at[lax.rem(step, 2)]


def derivatives(x_ref, u_ref, p, stream, step):
    x = x_ref[...]
    wg = stream.wait(0, step)
    pre_gate = dot(x, wg[...])
    wu = stream.wait(1, step)
    pre_up = dot(x, wu[...])
    wd = stream.wait(2, step)
    back = dot(u_ref[...], wd[...])
    s = jax.nn.sigmoid(pre_gate)
    activated = pre_gate * s
    hidden = (activated * pre_up).astype(BF)
    scaled_back = p * back
    d_gate = (scaled_back * pre_up * s * (1.0 + pre_gate * (1.0 - s))).astype(BF)
    d_up = (scaled_back * activated).astype(BF)
    return d_gate, d_up, hidden, back, wg, wu


def pieces_of(total, size):
    return [(a, min(size, total - a)) for a in range(0, total, size)]


def own_body(packed, early, groups, cap_ref, routes_ref, tok_hbm, out_hbm, wg_hbm, wu_hbm, wd_hbm, *refs):
    acts_refs, refs = (refs[:3], refs[3:]) if early is None else (refs[:4], refs[4:])
    (part_hbm, prob_ref, xq_hbm, sq_hbm, filled_ref, part_ref, xq_ref, sq_ref, tok_ref, out_ref, x_ref, u_ref, p_ref,
     table_ref, acc_ref, wg_ref, wu_ref, wd_ref, sems, row_sems, out_sems) = refs
    step = pl.program_id(0)
    width, block = wg_ref.shape[1:]
    quarter = xq_ref.shape[1]
    stream = Stream((wg_hbm, wu_hbm, wd_hbm), (wg_ref, wu_ref, wd_ref), sems, block, wg_hbm.shape[1] // block)
    owner, _, group = my_place(part_ref.shape[0])
    half = part_ref.shape[0] // 2
    halves = [pltpu.make_async_copy(part_ref.at[k * half:(k + 1) * half], part_hbm.at[k * half:(k + 1) * half],
                                    out_sems.at[k]) for k in range(2)]
    shares_out = [pltpu.make_async_copy(xq_ref, xq_hbm, out_sems.at[2]),
                  pltpu.make_async_copy(sq_ref, sq_hbm, out_sems.at[3])]

    @pl.when(step == 0)
    def _():
        rows = [pltpu.make_async_copy(tok_hbm, tok_ref, row_sems.at[0]),
                pltpu.make_async_copy(out_hbm, out_ref, row_sems.at[1])]
        rows[0].start()
        stream.copy(0, 0).start()
        rows[1].start()
        stream.copy(1, 0).start()
        stream.copy(2, 0).start()
        table, p = slot_table(routes_ref[...].astype(F32), owner, cap_ref[owner], (group == 1) & (groups == 2))
        table_ref[...] = table.astype(BF)
        p_ref[...] = p
        filled_ref[...] = jnp.sum(table, axis=1, keepdims=True)
        acc_ref[...] = jnp.zeros_like(acc_ref)
        prob_ref[...] = jnp.zeros_like(prob_ref)
        rows[0].wait()
        x_ref[...] = dot(table_ref[...], tok_ref[...]).astype(BF)
        rows[1].wait()
        u_ref[...] = dot(table_ref[...], out_ref[...]).astype(BF)
        at = pl.ds(pl.multiple_of(group * quarter, quarter), quarter)
        xq_ref[...] = x_ref[:, at]
        sq_ref[...] = (p * u_ref[:, at].astype(F32)).astype(BF)
        for copy in shares_out:
            copy.start()

    stream.ahead(step)
    d_gate, d_up, hidden, back, wg, wu = derivatives(x_ref, u_ref, p_ref[...], stream, step)
    acts = (d_gate, d_up, hidden)

    def store_early():
        for ref, value in zip(acts_refs, acts):
            ref[...] = value

    if early is None:
        store_early()
    else:
        pl.when(step < early)(store_early)

        @pl.when(step >= early)
        def _():
            for i, value in enumerate(acts):
                acts_refs[3][i] = value

    prob_ref[...] += jnp.sum(hidden.astype(F32) * back, axis=1, keepdims=True)
    gate_t = d_gate.T
    up_t = d_up.T
    for a, n in pieces_of(width, 512):
        at = slice(a, a + n)
        acc_ref[at, :] += dot(wg[at, :], gate_t) + dot(wu[at, :], up_t)

    @pl.when(step == pl.num_programs(0) - 1)
    def _():
        table = table_ref[...]
        count = table.shape[1]
        shares, _, fw = part_ref.shape
        by_slot = (((0,), (1,)), ((), ()))
        if packed:
            total = prob_ref[...]
            high = total.astype(BF).astype(F32)
            lane = lax.broadcasted_iota(jnp.int32, (CAP, 128), 1)
            both = jnp.where(lane == 0, high, jnp.where(lane == 1, total - high, 0.0)).astype(BF)
            by_token = dotg(both, table, FIRST)[:EXTRA].astype(BF)
        for j in range(shares):
            part_ref[j, :count, :] = dotg(table, acc_ref[j * fw:(j + 1) * fw, :].astype(BF), by_slot).astype(BF)
            if packed:
                part_ref[j, count:, :] = jnp.zeros((EXTRA, fw), BF)
                part_ref[j, count:, :count] = by_token
            if (j + 1) % half == 0:
                halves[j // half].start()
        for copy in halves + shares_out:
            copy.wait()


def weight_slots(width, block):
    return [pltpu.VMEM((2, width, block), BF)] * 3 + [pltpu.SemaphoreType.DMA((3, 2))]


def own_group(capacity, routes, tokens, grad_out, wg, wu, wd, shares, groups, packed, block, early):
    count, width = tokens.shape
    hidden = wg.shape[1]
    steps = hidden // block
    tall = count + (EXTRA if packed else 0)
    fw = width // shares
    quarter = width // groups
    act_specs = [pl.BlockSpec((CAP, block), lambda j: (0, jnp.minimum(j, early - 1)))] * 3
    acts = [pltpu.HBM((CAP, early * block), BF)] * 3
    if early < steps:
        act_specs.append(pl.BlockSpec((3, CAP, block), lambda j: (0, 0, jnp.maximum(j - early, 0))))
        acts.append(pltpu.HBM((3, CAP, (steps - early) * block), BF))
    column = pltpu.HBM((CAP, 1), F32)
    share = pltpu.HBM((CAP, quarter), BF)
    part = pltpu.HBM((shares, tall, fw), BF)
    rows = pltpu.VMEM((CAP, width), BF)
    tall_rows = pltpu.VMEM((count, width), BF)
    return pl.pallas_call(
        functools.partial(own_body, packed, early if early < steps else None, groups),
        grid=(steps,),
        in_specs=[whole_smem(), whole(routes.shape)] + [in_place()] * 5,
        out_specs=act_specs + [in_place(), whole(column.shape), in_place(), in_place(), whole(column.shape)],
        out_shape=acts + [part, column, share, share, column],
        scratch_shapes=[pltpu.VMEM(part.shape, BF)] + [pltpu.VMEM(share.shape, BF)] * 2 + [tall_rows, tall_rows, rows, rows, pltpu.VMEM((CAP, 1), F32), pltpu.VMEM((CAP, count), BF),
                        pltpu.VMEM((width, CAP), F32)] + weight_slots(width, block)
        + [pltpu.SemaphoreType.DMA((2,)), pltpu.SemaphoreType.DMA((4,))],
        compiler_params=params(46),
        cost_estimate=pl.CostEstimate(
            flops=10 * CAP * width * hidden, bytes_accessed=6 * width * hidden, transcendentals=CAP * hidden),
        name="own_group",
    )(capacity, pltpu.with_memory_space_constraint(routes, pltpu.HBM), tokens, grad_out, wg, wu, wd)


def joined(mine, other):
    return jnp.concatenate([mine, other], axis=0)


def merged(group, mine, other):
    first, last = jnp.where(group == 0, mine, other), jnp.where(group == 0, other, mine)
    lead = SHORT - CAP
    shared = CAP - lead
    return jnp.concatenate([first[:lead], first[lead:] + last[:shared], last[shared:]], axis=0)


def store_grads(groups, group, fits_ref, xs_ref, ss_ref, mine, other, out_refs):
    def grads(join, rows):
        for i, (rows_ref, out_ref) in enumerate(zip((xs_ref, xs_ref, ss_ref), out_refs)):
            out_ref[...] = dotg(rows_ref[:rows, :], join(mine(i), other(i)), FIRST).astype(BF)

    if groups == 2:
        @pl.when(fits_ref[0] == 1)
        def _():
            grads(functools.partial(merged, group), SHORT)

    @pl.when(fits_ref[0] == 0)
    def _():
        grads(joined, xs_ref.shape[0])


def again_body(groups, shares, steps, cap_ref, xq_ref, sq_ref, filled_ref, one_hbm, two_hbm, dg_ref, du_ref, h_ref,
               wg_hbm, wu_hbm, wd_hbm, gg_ref, gu_ref, gd_ref, xs_hbm, ss_hbm, fits_ref,
               xs_ref, ss_ref, one_ref, two_ref, xo_ref, uo_ref, po_ref, wg_ref, wu_ref, wd_ref, sems, row_sems):
    step = pl.program_id(0)
    owner, parity, group = my_place(shares)
    quarter = xs_ref.shape[1]
    count = one_ref.shape[1] - EXTRA
    stream = Stream((wg_hbm, wu_hbm, wd_hbm), (wg_ref, wu_ref, wd_ref), sems, wg_ref.shape[2], steps)
    joint = [pltpu.make_async_copy(xs_ref, xs_hbm, row_sems.at[2]), pltpu.make_async_copy(ss_ref, ss_hbm, row_sems.at[3])]

    @pl.when(step == 0)
    def _():
        rows = [pltpu.make_async_copy(one_hbm, one_ref, row_sems.at[0]),
                pltpu.make_async_copy(two_hbm, two_ref, row_sems.at[1])]
        for copy in rows:
            copy.start()
        stream.first()
        for copy in rows:
            copy.wait()
        filled = jnp.sum(filled_ref[...])
        for g in range(groups - 1):
            at = slice(g * CAP, (g + 1) * CAP)
            routes = one_ref[g, count:count + EXTRA, :count].astype(F32)
            table, p = slot_table(routes, owner, cap_ref[owner], (group == 0) & (groups == 2))
            filled += jnp.sum(table)
            po_ref[at, :] = p
            table = table.astype(BF)
            from_one = dot(table, one_ref[g, :count, :]).astype(BF)
            from_two = dot(table, two_ref[g, :count, :]).astype(BF)

            @pl.when(parity == 0)
            def _():
                xo_ref[at, :] = from_one
                uo_ref[at, :] = from_two

            @pl.when(parity == 1)
            def _():
                xo_ref[at, :] = from_two
                uo_ref[at, :] = from_one

        fits = filled <= SHORT if groups == 2 else jnp.bool_(False)
        fits_ref[0] = fits.astype(jnp.int32)
        part = pl.ds(pl.multiple_of(group * quarter, quarter), quarter)
        mine, scaled = xq_ref[...], sq_ref[...]
        other = xo_ref[:, part]
        scaled_other = (po_ref[...] * uo_ref[:, part].astype(F32)).astype(BF)
        if groups == 2:
            @pl.when(fits)
            def _():
                xs_ref[:SHORT, :] = merged(group, mine, other)
                ss_ref[:SHORT, :] = merged(group, scaled, scaled_other)

        @pl.when(jnp.logical_not(fits))
        def _():
            xs_ref[...] = joined(mine, other)
            ss_ref[...] = joined(scaled, scaled_other)

        for copy in joint:
            copy.start()

    stream.ahead(step)
    acts = derivatives(xo_ref, uo_ref, po_ref[...], stream, step)
    own = (dg_ref, du_ref, h_ref)
    store_grads(groups, group, fits_ref, xs_ref, ss_ref, lambda i: own[i][...], lambda i: acts[i], (gg_ref, gu_ref, gd_ref))

    @pl.when(step == steps - 1)
    def _():
        for copy in joint:
            copy.wait()


def grads_again(capacity, xq, sq, filled, one, two, dg, du, h, wg, wu, wd, groups, shares, block):
    width, hidden = wg.shape
    others = (groups - 1) * CAP
    quarter = width // groups
    steps = dg.shape[1] // block
    act = pl.BlockSpec((CAP, block), lambda j: (0, j))
    grad = pl.BlockSpec((quarter, block), lambda j: (0, j))
    arrived = pltpu.VMEM(one.shape, BF)
    rows = pltpu.VMEM((others, width), BF)
    joint = jax.ShapeDtypeStruct((CAP + others, quarter), BF)
    return pl.pallas_call(
        functools.partial(again_body, groups, shares, steps),
        grid=(steps,),
        in_specs=[whole_smem(), whole(xq.shape), whole(sq.shape), whole(filled.shape), in_place(), in_place(),
                  act, act, act, in_place(), in_place(), in_place()],
        out_specs=[grad] * 3 + [in_place()] * 2 + [whole_smem()],
        out_shape=[jax.ShapeDtypeStruct((quarter, hidden), BF)] * 3 + [joint] * 2 + [jax.ShapeDtypeStruct((1,), jnp.int32)],
        scratch_shapes=[pltpu.VMEM(joint.shape, BF)] * 2 + [arrived, arrived, rows, rows, pltpu.VMEM((others, 1), F32)]
        + weight_slots(width, block) + [pltpu.SemaphoreType.DMA((4,))],
        compiler_params=params(),
        cost_estimate=pl.CostEstimate(
            flops=(6 * others * width + 6 * (CAP + others) * quarter) * steps * block,
            bytes_accessed=6 * (width + quarter) * steps * block, transcendentals=others * steps * block),
        name="grads_again",
    )(capacity, xq, sq, filled, one, two, dg, du, h, wg, wu, wd)


def given_body(groups, shares, fits_ref, xs_ref, ss_ref, mine_ref, other_ref, gg_in, gu_in, gd_in, gg_ref, gu_ref, gd_ref):
    _, _, group = my_place(shares)
    store_grads(groups, group, fits_ref, xs_ref, ss_ref, lambda i: mine_ref[i], lambda i: other_ref[i], (gg_ref, gu_ref, gd_ref))


def grads_given(fits, xs, ss, mine, other, grads, groups, shares, block):
    quarter, hidden = grads[0].shape
    steps = mine.shape[2] // block
    early = hidden // block - steps
    grad = pl.BlockSpec((quarter, block), lambda j: (0, j + early))
    act = pl.BlockSpec((3, CAP, block), lambda j: (0, 0, j))
    return pl.pallas_call(
        functools.partial(given_body, groups, shares),
        grid=(steps,),
        in_specs=[whole_smem(), whole(xs.shape), whole(ss.shape), act, act] + [in_place()] * 3,
        out_specs=[grad] * 3,
        out_shape=[jax.ShapeDtypeStruct((quarter, hidden), BF)] * 3,
        input_output_aliases={5: 0, 6: 1, 7: 2},
        compiler_params=params(),
        cost_estimate=pl.CostEstimate(
            flops=6 * xs.shape[0] * quarter * steps * block, bytes_accessed=6 * quarter * steps * block, transcendentals=0),
        name="grads_given",
    )(fits, xs, ss, mine, other, *grads)


def block_of(hidden, largest):
    for size in (512, 256, 128):
        if size <= largest and hidden % size == 0:
            return size
    return hidden


def per_device(tokens, grad_out, gate_probs, expert_ids, capacity, w_gate, w_up, w_down):
    groups = lax.axis_size("expert")
    shares = lax.axis_size("dp")
    count, width = tokens.shape
    hidden = w_gate.shape[1]
    per_expert = shares // EXPERTS
    packed = width // shares >= count
    block = block_of(hidden, 512)
    steps = hidden // block
    early = steps - steps * 3 // 7 if groups == 2 else steps

    routes, send = pack(expert_ids.T, gate_probs.T, tokens, grad_out, shares)
    arounds = [[(i, (i + shift) % groups) for i in range(groups)] for shift in range(1, groups)]
    one = [lax.ppermute(send, "expert", around) for around in arounds]

    *acts, part, prob, xq, sq, filled = own_group(
        capacity, routes, tokens, grad_out, w_gate, w_up, w_down, shares, groups, packed, block, early)

    one, part = lax.optimization_barrier((one, part))
    swap = [(i, i ^ 1) for i in range(shares)]
    two = [lax.ppermute(rows, "dp", swap) for rows in one]
    if early < steps:
        late = acts.pop()
        late_other = lax.ppermute(late, "expert", arounds[0])
    arrived = lax.all_to_all(part, "dp", split_axis=0, concat_axis=0, tiled=True)

    def stacked(parts):
        return parts[0][None] if len(parts) == 1 else jnp.stack(parts)

    *grads, xs, ss, fits = grads_again(
        capacity, xq, sq, filled, stacked(one), stacked(two), *acts, w_gate, w_up, w_down, groups, shares, block)
    if early < steps:
        grads = grads_given(fits, xs, ss, late, late_other, grads, groups, shares, block)
    grad_gate, grad_up, grad_down = grads

    token_grad = jnp.sum(arrived[:, :count].astype(F32), axis=0).astype(BF)
    if packed:
        ends = arrived[:, count:count + 2, :count].astype(F32)
        by_expert = jnp.sum(ends.reshape(EXPERTS, per_expert * 2, count), axis=1)
    else:
        owner, _, group = my_place(shares)
        table, _ = slot_table(routes.astype(F32), owner, capacity[owner], (group == 1) & (groups == 2))
        mine = jnp.sum(table * prob, axis=0)
        one_hot = (jnp.arange(EXPERTS) == owner).astype(F32)
        by_expert = lax.psum(one_hot[:, None] * mine[None, :], "dp")
    match = expert_ids[:, :, None] == jnp.arange(EXPERTS, dtype=jnp.int32)
    prob_grad = jnp.sum(jnp.where(match, by_expert.T[:, None, :], 0.0), axis=2).astype(BF)
    return (token_grad, prob_grad, grad_gate, grad_up, grad_down)


def solution(mesh):
    return jax.shard_map(
        per_device,
        mesh=mesh,
        in_specs=(
            P("expert", None),
            P("expert", None),
            P("expert", None),
            P("expert", None),
            P(),
            P(None, "dp"),
            P(None, "dp"),
            P(None, "dp"),
        ),
        out_specs=(
            P("expert", "dp"),
            P("expert", None),
            P("expert", "dp"),
            P("expert", "dp"),
            P("expert", "dp"),
        ),
        check_vma=False,
    )
```
